512 devices in a mesh: seq: 128 (over y, z, x_lo), grp: 4 (over x_hi, core).
Axes of the slice: x: 4 (x_hi: 2, x_lo: 2; x = x_hi * 2 + x_lo), y: 4, z: 16, core: 2. Of those that a mesh axis runs over, the one named last changes fastest.
Arguments:
- query_main: bfloat16 [12288, 2560], P('seq', 'grp'), may hold values from -7 to 7
- key_main: bfloat16 [12288, 2560], P('seq', 'grp'), may hold values from -9 to 9
- value_main: bfloat16 [12288, 2560], P('seq', 'grp'), may hold values from -6 to 6
- query_guide: bfloat16 [12288, 1536], P('seq', 'grp'), may hold values from -7 to 7
- key_guide: bfloat16 [12288, 1536], P('seq', 'grp'), may hold values from -9 to 9
- value_guide: bfloat16 [12288, 1536], P('seq', 'grp'), may hold values from -6 to 6
- map_main: bfloat16 [2560, 64], P('grp'), may hold values from -0.47851562 to 0.47851562
- map_guide: bfloat16 [1536, 64], P('grp'), may hold values from -0.47851562 to 0.47851562
Outputs:
- guided: float32 [12288, 64], P('seq')
The draws below stay inside these ranges and needn't reach their ends.
All inputs are finite; a program needn't handle non-finite values.
Results may differ from the reference program's by a relative error of at most 0.0065.
Values may be sent and summed in bfloat16 or wider, within the bound.
No kernel may reach another device: no remote copies, remote signals or barrier semaphores. Data moves between devices by JAX's collectives and lax.ppermute only.
A program may use at most 64 MiB of HBM per device.

```python
import math
import jax
import jax.numpy as jnp
from jax import lax

HD = 128
H_MAIN = 20
H_GUIDE = 12
CH = 64
TOK_DEV = 96
TOKENS = 12288
HG = 8


def draw_query_main(key, part):
    key = jax.random.fold_in(key, 1)
    entries = jnp.clip(1.5 * jax.random.normal(key, (TOKENS, H_MAIN, HD), jnp.float32), -6.0, 6.0)
    return entries.reshape(TOKENS, H_MAIN * HD).astype(jnp.bfloat16)


def draw_key_main(key, part):
    key = jax.random.fold_in(key, 2)
    entries = jnp.clip(1.5 * jax.random.normal(key, (TOKENS, H_MAIN, HD), jnp.float32), -6.0, 6.0)
    return entries.reshape(TOKENS, H_MAIN * HD).astype(jnp.bfloat16)


def draw_query_guide(key, part):
    key = jax.random.fold_in(key, 3)
    entries = jnp.clip(1.5 * jax.random.normal(key, (TOKENS, H_GUIDE, HD), jnp.float32), -6.0, 6.0)
    return entries.reshape(TOKENS, H_GUIDE * HD).astype(jnp.bfloat16)


def draw_key_guide(key, part):
    key = jax.random.fold_in(key, 4)
    entries = jnp.clip(1.5 * jax.random.normal(key, (TOKENS, H_GUIDE, HD), jnp.float32), -6.0, 6.0)
    return entries.reshape(TOKENS, H_GUIDE * HD).astype(jnp.bfloat16)


def steps_of(stream_key, dims, split, least, largest):
    def one(position, shards_of):
        steps = jax.random.uniform(jax.random.fold_in(jax.random.fold_in(stream_key, 6), position), (shards_of,), jnp.float32, least / len(split), largest / len(split))
        return jnp.repeat(jnp.exp(steps), dims[position] // shards_of).reshape((-1,) + (1,) * (len(dims) - position - 1))

    gain = one(*split[0])
    for cut in split[1:]:
        gain = gain * one(*cut)
    return gain


def bell_draw(own_key, shape, width, reach, shards=(), held_as=jnp.bfloat16):
    array = width * jax.random.normal(own_key, shape, jnp.float32)
    if shards:
        array = array * steps_of(own_key, shape, shards, -0.22, 0.18)
    return jnp.clip(array, -reach, reach).astype(held_as)


def setup_inputs(seed: int = 0) -> dict:
    key_of = jax.random.split(jax.random.key(seed), 9)
    return {
        "query_main": draw_query_main(jax.random.fold_in(key_of[8], 71), 0),
        "key_main": draw_key_main(jax.random.fold_in(key_of[8], 71), 0),
        "value_main": bell_draw(key_of[2], (TOKENS, H_MAIN * HD), 1.0, 6.0, ((0, 128), (1, 4))),
        "query_guide": draw_query_guide(jax.random.fold_in(key_of[8], 71), 0),
        "key_guide": draw_key_guide(jax.random.fold_in(key_of[8], 71), 0),
        "value_guide": bell_draw(key_of[5], (TOKENS, H_GUIDE * HD), 1.0, 6.0, ((0, 128), (1, 4))),
        "map_main": bell_draw(key_of[6], (H_MAIN * HD, CH), 0.08, 0.47851562, ((0, 4),)),
        "map_guide": bell_draw(key_of[7], (H_GUIDE * HD, CH), 0.08, 0.47851562, ((0, 4),)),
    }


guidance = 2.5

def head_attention(queries, keys_all, values_all):
    scaling = 1.0 / math.sqrt(HD)
    block_rows = HG * TOK_DEV
    blocks = queries.reshape(TOKENS // block_rows, block_rows, HD)

    def attend_rows(query_block):
        scores = jnp.dot(query_block, keys_all.T, preferred_element_type=jnp.float32) * scaling
        highest = lax.optimization_barrier(jnp.max(scores, axis=1, keepdims=True))
        weights = jnp.exp(scores - highest)
        summed = lax.optimization_barrier(jnp.sum(weights, axis=1, keepdims=True))
        output = jnp.dot(weights.astype(jnp.bfloat16), values_all, preferred_element_type=jnp.float32) / summed
        return output.astype(jnp.bfloat16)
    return lax.map(attend_rows, blocks).reshape(TOKENS, HD)

def all_heads(queries, keys_all, values_all, head_count):

    def by_heads(matrix):
        return matrix.reshape(TOKENS, head_count, HD).transpose(1, 0, 2)
    outputs = lax.map(lambda triple: head_attention(triple[0], triple[1], triple[2]), (by_heads(queries), by_heads(keys_all), by_heads(values_all)))
    return outputs.transpose(1, 0, 2).reshape(TOKENS, head_count * HD)

def reference(query_main, key_main, value_main, query_guide, key_guide, value_guide, map_main, map_guide):
    out_main = all_heads(query_main, key_main, value_main, H_MAIN)
    out_guide = all_heads(query_guide, key_guide, value_guide, H_GUIDE)
    main_pred = jnp.dot(out_main, map_main, preferred_element_type=jnp.float32)
    guide_pred = jnp.dot(out_guide, map_guide, preferred_element_type=jnp.float32)
    return guide_pred + guidance * (main_pred - guide_pred)
```

```python
import functools
import math

import jax
import jax.numpy as jnp
from jax import lax
from jax.experimental import pallas as pl
from jax.experimental.pallas import tpu as pltpu
from jax.sharding import Mesh
from jax.sharding import PartitionSpec as P

HD = 128
CH = 64
guidance = 2.5
SCALE = math.log2(math.e) / math.sqrt(HD)
F32 = jnp.float32
BF16 = jnp.bfloat16
VMEM = pl.BlockSpec(memory_space=pltpu.VMEM)
MESSAGE_ROWS = CH + 16

SEQ = ("y", "zh", "z0", "xl")
GRP = ("xh", "c")
Z = ("zh", "z0")
QUERY_AXES = ("z0", "xl")


def dot_t(a, b):
    return lax.dot_general(a, b, (((1,), (1,)), ((), ())), preferred_element_type=F32)


def pack_kernel(half, main_heads, guide_heads, qm, km, vm, qg, kg, vg, q_out, kv_out):
    for h in range(main_heads + guide_heads):
        if h < main_heads:
            q, k, v, at = qm, km, vm, h * HD
        else:
            q, k, v, at = qg, kg, vg, (h - main_heads) * HD
        for b in range(2):
            rows = slice(b * half, (b + 1) * half)
            q_out[2 * h + b] = q[rows, at : at + HD]
            kv_out[2 * h + b, 0] = k[rows, at : at + HD]
            kv_out[2 * h + b, 1] = v[rows, at : at + HD]


def split_two(x):
    high = x.astype(BF16).astype(F32)
    return high, x - high


def attend_kernel(rows_at_once, q_ref, *refs):
    *kv_refs, map_ref, out_ref, sums_ref = refs
    rows = out_ref.shape[2]
    keys = kv_refs[0].shape[0] * kv_refs[0].shape[2]
    ones = jnp.ones((keys, HD), BF16)
    lane = lax.broadcasted_iota(jnp.int32, (rows_at_once, HD), 1)
    picks = lax.broadcasted_iota(jnp.int32, (16, HD), 0) == lax.broadcasted_iota(
        jnp.int32, (16, HD), 1
    )
    picks = picks.astype(F32).astype(BF16)

    def block(piece):
        return piece[:, 0].reshape(keys, HD), piece[:, 1].reshape(keys, HD)

    def weighted(queries, shift):
        total = None
        for piece in kv_refs:
            k, v = block(piece)
            scores = dot_t(queries, k) * SCALE
            if shift is not None:
                scores = scores - shift
            weights = jnp.exp2(scores).astype(BF16)
            part = jnp.dot(
                weights, jnp.concatenate([v, ones], axis=1), preferred_element_type=F32
            )
            total = part if total is None else total + part
        return total

    def highest(queries):
        top = None
        for piece in kv_refs:
            k, _ = block(piece)
            here = jnp.max(dot_t(queries, k), axis=1, keepdims=True)
            top = here if top is None else jnp.maximum(top, here)
        return jnp.ceil(top * SCALE)

    def emit(at, total, shift):
        out_ref[0, :CH, at] = dot_t(map_ref[...], total[:, :HD].astype(BF16)).astype(BF16)
        high, low = split_two(total[:, HD:])
        rest = jnp.where(lane == 0, high, jnp.where(lane == 1, low, 0.0))
        if shift is not None:
            high, low = split_two(shift)
            rest = jnp.where(lane == 2, high, jnp.where(lane == 3, low, rest))
        out_ref[0, CH:, at] = dot_t(picks, rest.astype(BF16)).astype(BF16)

    for i in range(rows // rows_at_once):
        at = slice(i * rows_at_once, (i + 1) * rows_at_once)
        total = weighted(q_ref[at, :], None)
        emit(at, total, None)
        sums_ref[at, :] = total[:, HD:]
    least = jnp.min(sums_ref[...])
    most = jnp.max(sums_ref[...])

    @pl.when(jnp.logical_not((least > 1e-20) & (most < 1e25)))
    def _():
        @pl.loop(0, rows // rows_at_once)
        def _(i):
            at = pl.ds(pl.multiple_of(i * rows_at_once, rows_at_once), rows_at_once)
            queries = q_ref[at, :]
            shift = highest(queries)
            emit(at, weighted(queries, shift), shift)


def attend(queries, key_values, map_t, rows, rows_at_once=256):
    blocks = queries.shape[0] // rows
    keys = key_values[0].shape[0] * key_values[0].shape[2] * len(key_values)
    whole = pl.BlockSpec(key_values[0].shape, lambda i: (0, 0, 0, 0))
    return pl.pallas_call(
        functools.partial(attend_kernel, rows_at_once),
        grid=(blocks,),
        in_specs=[pl.BlockSpec((rows, HD), lambda i: (i, 0))]
        + [whole] * len(key_values)
        + [pl.BlockSpec((CH, HD), lambda i: (0, 0))],
        out_specs=pl.BlockSpec((1, MESSAGE_ROWS, rows), lambda i: (i, 0, 0)),
        out_shape=jax.ShapeDtypeStruct((blocks, MESSAGE_ROWS, rows), BF16),
        scratch_shapes=[pltpu.VMEM((rows, HD), F32)],
        compiler_params=pltpu.CompilerParams(vmem_limit_bytes=40 << 20),
        cost_estimate=pl.CostEstimate(
            flops=4 * queries.shape[0] * keys * HD,
            bytes_accessed=3 << 20,
            transcendentals=queries.shape[0] * keys,
        ),
    )(queries, *key_values, map_t)


def combine_kernel(gain_ref, in_ref, out_ref):
    parts = in_ref.shape[0]
    tokens = 2 * out_ref.shape[1]
    stats = [in_ref[p, CH:, :].astype(F32) for p in range(parts)]
    shifts = [s[2:3] + s[3:4] for s in stats]
    top = functools.reduce(jnp.maximum, shifts)
    scales = [jnp.exp2(shift - top) for shift in shifts]
    summed = sum((s[0:1] + s[1:2]) * scale for s, scale in zip(stats, scales))
    velocity = sum(in_ref[p, :CH, :].astype(F32) * scale for p, scale in enumerate(scales))
    velocity = (velocity * (gain_ref[0] / summed)).T
    velocity = velocity.reshape(out_ref.shape[0], 2, tokens // 2, CH)
    out_ref[...] = jnp.concatenate([velocity[:, 0], velocity[:, 1]], axis=2).astype(BF16)


def body(
    query_main, key_main, value_main, query_guide, key_guide, value_guide, map_main, map_guide
):
    tokens_here = query_main.shape[0]
    half = tokens_here // 2
    main_heads = query_main.shape[1] // HD
    guide_heads = query_guide.shape[1] // HD
    planes = lax.axis_size(Z)
    head = lax.axis_index("zh")

    maps = jnp.concatenate([map_main, map_guide], axis=0).reshape(-1, HD, CH)
    map_t = lax.dynamic_index_in_dim(maps, head, 0, keepdims=False).T
    gain = jnp.where(head < main_heads, guidance, 1.0 - guidance).astype(F32).reshape(1)

    with jax.named_scope("pack"):
        q, kv = pl.pallas_call(
            functools.partial(pack_kernel, half, main_heads, guide_heads),
            in_specs=[VMEM] * 6,
            out_specs=[VMEM] * 2,
            out_shape=[
                jax.ShapeDtypeStruct((planes, half, HD), BF16),
                jax.ShapeDtypeStruct((planes, 2, half, HD), BF16),
            ],
        )(query_main, key_main, value_main, query_guide, key_guide, value_guide)
    with jax.named_scope("to_heads"):
        q = lax.all_to_all(q, Z, 0, 0, tiled=True)
        kv = lax.all_to_all(kv, Z, 0, 0, tiled=True)
    rows = planes * half
    with jax.named_scope("gather"):
        queries = lax.all_gather(q.reshape(rows, HD), QUERY_AXES, axis=0, tiled=True)
        around = lax.axis_size("y")
        key_values = [kv] + [
            lax.ppermute(kv, "y", [(i, (i + by) % around) for i in range(around)])
            for by in (1, around - 1, 2)
        ]
    with jax.named_scope("attend"):
        shares = attend(queries, key_values, map_t, rows)
    with jax.named_scope("combine"):
        shares = lax.all_to_all(shares, QUERY_AXES, 0, 0, tiled=True)
        velocity = pl.pallas_call(
            combine_kernel,
            in_specs=[pl.BlockSpec(memory_space=pltpu.SMEM), VMEM],
            out_specs=VMEM,
            out_shape=jax.ShapeDtypeStruct((planes, half // 2, 2 * CH), BF16),
        )(gain, shares)
    with jax.named_scope("to_tokens"):
        velocity = lax.all_to_all(velocity, Z, 0, 0, tiled=True)
        velocity = jnp.sum(
            velocity.reshape(planes // 2, half, 2 * CH).astype(F32), axis=0
        )
        everywhere = lax.all_gather(velocity, GRP, axis=0)
        velocity = jnp.sum(everywhere, axis=0)
    return velocity.reshape(2, half // 2, 2, CH).transpose(0, 2, 1, 3).reshape(tokens_here, CH)


def solution(mesh):
    fine = Mesh(mesh.devices.reshape(4, 8, 2, 2, 2, 2), SEQ + GRP)
    placed = (P(SEQ, GRP),) * 6 + (P(GRP, None),) * 2
    return jax.shard_map(
        body, mesh=fine, in_specs=placed, out_specs=P(SEQ, None), check_vma=False
    )
```

```python
import functools
import math

import jax
import jax.numpy as jnp
from jax import lax
from jax.experimental import pallas as pl
from jax.experimental.pallas import tpu as pltpu
from jax.sharding import Mesh
from jax.sharding import PartitionSpec as P

HD = 128
CH = 64
guidance = 2.5
SCALE = math.log2(math.e) / math.sqrt(HD)
F32 = jnp.float32
BF16 = jnp.bfloat16
VMEM = pl.BlockSpec(memory_space=pltpu.VMEM)
SMEM = pl.BlockSpec(memory_space=pltpu.SMEM)
SMALL = pltpu.CompilerParams(vmem_limit_bytes=12 << 20)
MESSAGE_ROWS = CH + 16

SEQ = ("y", "zh", "z0", "xl")
GRP = ("xh", "c")
QUERY_AXES = ("z0", "xl")


def dot_t(a, b):
    return lax.dot_general(a, b, (((1,), (1,)), ((), ())), preferred_element_type=F32)


def pack_kernel(main_heads, guide_heads, qm, km, vm, qg, kg, vg, out_ref):
    for h in range(main_heads + guide_heads):
        at = (h if h < main_heads else h - main_heads) * HD
        for t, ref in enumerate((qm, km, vm) if h < main_heads else (qg, kg, vg)):
            out_ref[h, t] = ref[:, at : at + HD]


def split_two(x):
    high = x.astype(BF16).astype(F32)
    return high, x - high


def attend_kernel(member, q_refs, kv_refs, map_ref, before_ref, out_ref, sums_ref):
    keys = kv_refs[0].shape[0] * kv_refs[0].shape[2]
    rows = out_ref.shape[2]
    last = out_ref.dtype == BF16
    ones = jnp.ones((keys, HD), BF16)
    lane = lax.broadcasted_iota(jnp.int32, (rows, HD), 1)
    picks = lax.broadcasted_iota(jnp.int32, (16, HD), 0) == lax.broadcasted_iota(
        jnp.int32, (16, HD), 1
    )
    picks = picks.astype(F32).astype(BF16)

    def block(piece):
        return piece[:, 0].reshape(keys, HD), piece[:, 1].reshape(keys, HD)

    def weighted(queries, shift):
        total = None
        for piece in kv_refs:
            k, v = block(piece)
            scores = dot_t(queries, k) * SCALE
            if shift is not None:
                scores = scores - shift
            weights = jnp.exp2(scores).astype(BF16)
            part = jnp.dot(
                weights, jnp.concatenate([v, ones], axis=1), preferred_element_type=F32
            )
            total = part if total is None else total + part
        return total

    def highest(queries):
        top = None
        for piece in kv_refs:
            k, _ = block(piece)
            here = jnp.max(dot_t(queries, k), axis=1, keepdims=True)
            top = here if top is None else jnp.maximum(top, here)
        return jnp.ceil(top * SCALE)

    def emit(i, total, shift):
        velocity = dot_t(map_ref[...], total[:, :HD].astype(BF16))
        high, low = split_two(total[:, HD:])
        rest = jnp.where(lane == 0, high, jnp.where(lane == 1, low, 0.0))
        if shift is not None:
            high, low = split_two(shift)
            rest = jnp.where(lane == 2, high, jnp.where(lane == 3, low, rest))
        stats = dot_t(picks, rest.astype(BF16))
        summed = stats[0:1] + stats[1:2]
        top = stats[2:3] + stats[3:4]
        if before_ref is not None:
            top_before = before_ref[i, CH + 1 : CH + 2, :]
            both = jnp.maximum(top, top_before)
            scale, scale_before = jnp.exp2(top - both), jnp.exp2(top_before - both)
            velocity = velocity * scale + before_ref[i, :CH, :] * scale_before
            summed = summed * scale + before_ref[i, CH : CH + 1, :] * scale_before
            top = both
        to = member ^ i if last else i
        out_ref[to, :CH, :] = velocity.astype(out_ref.dtype)
        if last:
            tail = split_two(summed) + split_two(top)
        else:
            tail = (summed, top)
        filler = jnp.zeros((out_ref.shape[1] - CH - len(tail), rows), F32)
        out_ref[to, CH:, :] = jnp.concatenate(tail + (filler,), axis=0).astype(out_ref.dtype)

    for i, q_ref in enumerate(q_refs):
        queries = q_ref[...]
        total = weighted(queries, None)
        emit(i, total, None)
        sums_ref[...] = total[:, HD:]
        least = jnp.min(sums_ref[...])
        most = jnp.max(sums_ref[...])

        @pl.when(jnp.logical_not((least > 1e-20) & (most < 1e25)))
        def _():
            shift = highest(queries)
            emit(i, weighted(queries, shift), shift)


def attend(member, queries, key_values, map_t, before, last):
    rows = queries[0].shape[0]
    blocks = len(queries)
    keys = key_values[0].shape[0] * key_values[0].shape[2] * len(key_values)
    operands = [*queries, *key_values, map_t] + ([] if before is None else [before])

    def kernel(member_ref, *refs):
        q_refs, refs = refs[:blocks], refs[blocks:]
        kv_refs, refs = refs[: len(key_values)], refs[len(key_values) :]
        map_ref, refs = refs[0], refs[1:]
        before_ref = None
        if before is not None:
            before_ref, refs = refs[0], refs[1:]
        attend_kernel(member_ref[0], q_refs, kv_refs, map_ref, before_ref, *refs)

    out = (blocks, MESSAGE_ROWS, rows) if last else (blocks, CH + 8, rows)
    return pl.pallas_call(
        kernel,
        in_specs=[SMEM] + [VMEM] * len(operands),
        out_specs=VMEM,
        out_shape=jax.ShapeDtypeStruct(out, BF16 if last else F32),
        scratch_shapes=[pltpu.VMEM((rows, HD), F32)],
        compiler_params=pltpu.CompilerParams(vmem_limit_bytes=40 << 20),
        cost_estimate=pl.CostEstimate(
            flops=8 * blocks * rows * keys * HD,
            bytes_accessed=3 << 20,
            transcendentals=blocks * rows * keys,
        ),
    )(member, *operands)


def combine_kernel(gain_ref, in_ref, out_ref):
    parts = in_ref.shape[0]
    half = out_ref.shape[1]
    stats = [in_ref[p, CH:, :].astype(F32) for p in range(parts)]
    shifts = [s[2:3] + s[3:4] for s in stats]
    top = functools.reduce(jnp.maximum, shifts)
    scales = [jnp.exp2(shift - top) for shift in shifts]
    summed = sum((s[0:1] + s[1:2]) * scale for s, scale in zip(stats, scales))
    velocity = sum(in_ref[p, :CH, :].astype(F32) * scale for p, scale in enumerate(scales))
    velocity = (velocity * (gain_ref[0] / summed)).T
    velocity = velocity.reshape(out_ref.shape[0], 2, half, CH)
    out_ref[...] = jnp.concatenate([velocity[:, 0], velocity[:, 1]], axis=2).astype(BF16)


def body(
    query_main, key_main, value_main, query_guide, key_guide, value_guide, map_main, map_guide
):
    tokens_here = query_main.shape[0]
    main_heads = query_main.shape[1] // HD
    guide_heads = query_guide.shape[1] // HD
    heads = main_heads + guide_heads
    head = lax.axis_index("zh")

    maps = jnp.concatenate([map_main, map_guide], axis=0).reshape(-1, HD, CH)
    map_t = lax.dynamic_index_in_dim(maps, head, 0, keepdims=False).T
    gain = jnp.where(head < main_heads, guidance, 1.0 - guidance).astype(F32).reshape(1)

    with jax.named_scope("pack"):
        packed = pl.pallas_call(
            functools.partial(pack_kernel, main_heads, guide_heads),
            in_specs=[VMEM] * 6,
            out_specs=VMEM,
            out_shape=jax.ShapeDtypeStruct((heads, 3, tokens_here, HD), BF16),
            compiler_params=SMALL,
        )(query_main, key_main, value_main, query_guide, key_guide, value_guide)
    with jax.named_scope("to_heads"):
        arrived = lax.all_to_all(packed, "zh", 0, 0, tiled=True)
    rows = heads * tokens_here
    with jax.named_scope("gather"):
        q = arrived[:, 0].reshape(rows, HD)
        kv = arrived[:, 1:]
        queries = [q] + [
            lax.ppermute(q, QUERY_AXES, [(i, i ^ by) for i in range(4)]) for by in (1, 2, 3)
        ]
        around = lax.axis_size("y")
        key_values = [kv] + [
            lax.ppermute(kv, "y", [(i, (i + by) % around) for i in range(around)])
            for by in (1, around - 1, 2)
        ]
    with jax.named_scope("attend"):
        member = lax.axis_index(QUERY_AXES).reshape(1)
        shares = attend(member, queries, key_values[:1], map_t, None, False)
        shares = attend(member, queries, key_values[1:3], map_t, shares, False)
        shares = attend(member, queries, key_values[3:], map_t, shares, True)
    with jax.named_scope("combine"):
        shares = lax.all_to_all(shares, QUERY_AXES, 0, 0, tiled=True)
        velocity = pl.pallas_call(
            combine_kernel,
            in_specs=[SMEM, VMEM],
            out_specs=VMEM,
            out_shape=jax.ShapeDtypeStruct((heads, tokens_here // 2, 2 * CH), BF16),
            compiler_params=SMALL,
        )(gain, shares)
    with jax.named_scope("to_tokens"):
        velocity = lax.all_to_all(velocity, "zh", 0, 0, tiled=True)
        velocity = jnp.sum(velocity.astype(F32), axis=0)
        everywhere = lax.all_gather(velocity, GRP, axis=0)
        velocity = jnp.sum(everywhere, axis=0)
    return velocity.reshape(tokens_here // 2, 2, CH).transpose(1, 0, 2).reshape(tokens_here, CH)


def solution(mesh):
    fine = Mesh(mesh.devices.reshape(4, 8, 2, 2, 2, 2), SEQ + GRP)
    placed = (P(SEQ, GRP),) * 6 + (P(GRP, None),) * 2
    return jax.shard_map(
        body, mesh=fine, in_specs=placed, out_specs=P(SEQ, None), check_vma=False
    )
```

```python
import functools
import math

import jax
import jax.numpy as jnp
from jax import lax
from jax.experimental import pallas as pl
from jax.experimental.pallas import tpu as pltpu
from jax.sharding import Mesh
from jax.sharding import PartitionSpec as P

HD = 128
CH = 64
guidance = 2.5
SCALE = math.log2(math.e) / math.sqrt(HD)
F32 = jnp.float32
BF16 = jnp.bfloat16
VMEM = pl.BlockSpec(memory_space=pltpu.VMEM)
SMEM = pl.BlockSpec(memory_space=pltpu.SMEM)
SMALL = pltpu.CompilerParams(vmem_limit_bytes=12 << 20)
MESSAGE_ROWS = CH + 16

SEQ = ("y", "zh", "z0", "xl")
GRP = ("xh", "c")
Z = ("zh", "z0")
PLANE_SETS = ([0, 2, 4, 6, 9, 11, 13, 15], [1, 3, 5, 7, 8, 10, 12, 14])
QUERY_AXES = ("y", "z0")
QUERY_STEPS = (1, 6, 7)
KEY_AXES = ("y", "xl")
KEY_STEPS = (1, 2, 3)


def exchange(x):
    return lax.all_to_all(x, Z, 0, 0, tiled=True, axis_index_groups=PLANE_SETS)


def from_partners(x, axes, steps):
    size = lax.axis_size(axes)
    return [lax.ppermute(x, axes, [(i, i ^ step) for i in range(size)]) for step in steps]


def dot_t(a, b):
    return lax.dot_general(a, b, (((1,), (1,)), ((), ())), preferred_element_type=F32)


def pack_kernel(main_heads, guide_heads, qm, km, vm, qg, kg, vg, q_out, kv_out):
    for h in range(main_heads + guide_heads):
        at = (h if h < main_heads else h - main_heads) * HD
        q, k, v = (qm, km, vm) if h < main_heads else (qg, kg, vg)
        q_out[h] = q[:, at : at + HD]
        kv_out[h, 0] = k[:, at : at + HD]
        kv_out[h, 1] = v[:, at : at + HD]


def split_two(x):
    high = x.astype(BF16).astype(F32)
    return high, x - high


def attend_kernel(q_ref, *refs):
    *kv_refs, map_ref, out_ref, sums_ref = refs
    rows = out_ref.shape[1]
    keys = kv_refs[0].shape[0] * kv_refs[0].shape[2]

    def all_pieces(which):
        return jnp.concatenate([ref[:, which].reshape(keys, HD) for ref in kv_refs], axis=0)

    def weighted(queries, shift):
        scores = dot_t(queries, all_pieces(0)) * SCALE
        if shift is not None:
            scores = scores - shift
        values = all_pieces(1)
        values = jnp.concatenate([values, jnp.ones_like(values)], axis=1)
        weights = jnp.exp2(scores).astype(BF16)
        return jnp.dot(weights, values, preferred_element_type=F32)

    def emit(at, total, shift):
        count = total.shape[0]
        lane = lax.broadcasted_iota(jnp.int32, (count, HD), 1)
        picks = lax.broadcasted_iota(jnp.int32, (16, HD), 0) == lax.broadcasted_iota(
            jnp.int32, (16, HD), 1
        )
        out_ref[:CH, at] = dot_t(map_ref[...], total[:, :HD].astype(BF16)).astype(BF16)
        high, low = split_two(total[:, HD:])
        rest = jnp.where(lane == 0, high, jnp.where(lane == 1, low, 0.0))
        if shift is not None:
            high, low = split_two(shift)
            rest = jnp.where(lane == 2, high, jnp.where(lane == 3, low, rest))
        rest = dot_t(picks.astype(F32).astype(BF16), rest.astype(BF16))
        out_ref[CH:, at] = rest.astype(BF16)

    total = weighted(q_ref[...], None)
    emit(slice(None), total, None)
    sums_ref[...] = total[:, HD:]
    least = jnp.min(sums_ref[...])
    most = jnp.max(sums_ref[...])

    @pl.when(jnp.logical_not((least > 1e-20) & (most < 1e25)))
    def _():
        @pl.loop(0, rows // HD)
        def _(i):
            at = pl.ds(pl.multiple_of(i * HD, HD), HD)
            queries = q_ref[at, :]
            top = jnp.max(dot_t(queries, all_pieces(0)), axis=1, keepdims=True)
            shift = jnp.ceil(top * SCALE)
            emit(at, weighted(queries, shift), shift)


def attend(queries, key_values, map_t):
    rows = queries.shape[0]
    keys = key_values[0].shape[0] * key_values[0].shape[2] * len(key_values)
    return pl.pallas_call(
        attend_kernel,
        in_specs=[VMEM] * (2 + len(key_values)),
        out_specs=VMEM,
        out_shape=jax.ShapeDtypeStruct((MESSAGE_ROWS, rows), BF16),
        scratch_shapes=[pltpu.VMEM((rows, HD), F32)],
        compiler_params=pltpu.CompilerParams(vmem_limit_bytes=40 << 20),
        cost_estimate=pl.CostEstimate(
            flops=8 * rows * keys * HD, bytes_accessed=2 << 20, transcendentals=rows * keys
        ),
    )(queries, *key_values, map_t)


def combine_kernel(gain_ref, *refs):
    *in_refs, out_ref = refs
    half = out_ref.shape[1]
    stats = [ref[CH:, :].astype(F32) for ref in in_refs]
    shifts = [s[2:3] + s[3:4] for s in stats]
    top = functools.reduce(jnp.maximum, shifts)
    scales = [jnp.exp2(shift - top) for shift in shifts]
    summed = sum((s[0:1] + s[1:2]) * scale for s, scale in zip(stats, scales))
    velocity = sum(ref[:CH, :].astype(F32) * scale for ref, scale in zip(in_refs, scales))
    velocity = (velocity * (gain_ref[0] / summed)).T
    velocity = velocity.reshape(out_ref.shape[0], 2, half, CH)
    out_ref[...] = jnp.concatenate([velocity[:, 0], velocity[:, 1]], axis=2).astype(BF16)


def body(
    query_main, key_main, value_main, query_guide, key_guide, value_guide, map_main, map_guide
):
    tokens_here = query_main.shape[0]
    main_heads = query_main.shape[1] // HD
    guide_heads = query_guide.shape[1] // HD
    heads = main_heads + guide_heads
    head = lax.axis_index("zh")

    maps = jnp.concatenate([map_main, map_guide], axis=0).reshape(-1, HD, CH)
    map_t = lax.dynamic_index_in_dim(maps, head, 0, keepdims=False).T
    gain = jnp.where(head < main_heads, guidance, 1.0 - guidance).astype(F32).reshape(1)

    with jax.named_scope("pack"):
        q, kv = pl.pallas_call(
            functools.partial(pack_kernel, main_heads, guide_heads),
            in_specs=[VMEM] * 6,
            out_specs=[VMEM] * 2,
            out_shape=[
                jax.ShapeDtypeStruct((heads, tokens_here, HD), BF16),
                jax.ShapeDtypeStruct((heads, 2, tokens_here, HD), BF16),
            ],
        )(query_main, key_main, value_main, query_guide, key_guide, value_guide)
    with jax.named_scope("to_heads"):
        kv = exchange(kv)
        q = exchange(q).reshape(heads * tokens_here, HD)
    with jax.named_scope("gather"):
        key_values = [kv] + from_partners(kv, KEY_AXES, KEY_STEPS)
        queries = from_partners(q, QUERY_AXES, QUERY_STEPS)
    with jax.named_scope("attend"):
        shares = [
            from_partners(attend(piece, key_values, map_t), QUERY_AXES, (step,))[0]
            for piece, step in zip(queries, QUERY_STEPS)
        ]
        shares.append(attend(q, key_values, map_t))
    with jax.named_scope("combine"):
        velocity = pl.pallas_call(
            combine_kernel,
            in_specs=[SMEM] + [VMEM] * len(shares),
            out_specs=VMEM,
            out_shape=jax.ShapeDtypeStruct((heads, tokens_here // 2, 2 * CH), BF16),
            compiler_params=SMALL,
        )(gain, *shares)
    with jax.named_scope("to_tokens"):
        velocity = jnp.sum(exchange(velocity).astype(F32), axis=0)
        everywhere = lax.all_gather(velocity, GRP, axis=0)
        velocity = jnp.sum(everywhere, axis=0)
    return velocity.reshape(tokens_here // 2, 2, CH).transpose(1, 0, 2).reshape(tokens_here, CH)


def solution(mesh):
    fine = Mesh(mesh.devices.reshape(4, 8, 2, 2, 2, 2), SEQ + GRP)
    placed = (P(SEQ, GRP),) * 6 + (P(GRP, None),) * 2
    return jax.shard_map(
        body, mesh=fine, in_specs=placed, out_specs=P(SEQ, None), check_vma=False
    )
```

```python
import functools
import math

import jax
import jax.numpy as jnp
from jax import lax
from jax.experimental import pallas as pl
from jax.experimental.pallas import tpu as pltpu
from jax.sharding import Mesh
from jax.sharding import PartitionSpec as P

HD = 128
CH = 64
guidance = 2.5
SCALE = math.log2(math.e) / math.sqrt(HD)
F32 = jnp.float32
BF16 = jnp.bfloat16
VMEM = pl.BlockSpec(memory_space=pltpu.VMEM)
SMEM = pl.BlockSpec(memory_space=pltpu.SMEM)
SMALL = pltpu.CompilerParams(vmem_limit_bytes=12 << 20)
MESSAGE_ROWS = CH + 16

SEQ = ("y", "zh", "z0", "xl")
GRP = ("xh", "c")
Z = ("zh", "z0")
PLANE_SETS = ([0, 2, 4, 6, 9, 11, 13, 15], [1, 3, 5, 7, 8, 10, 12, 14])
QUERY_AXES = ("y", "z0")
QUERY_STEPS = (1, 6, 7)
KEY_AXES = ("y", "xl")
KEY_SETS = ([0, 1, 2, 3], [4, 5, 6, 7])
SIDES = 2
PLANE_AXES = Z + ("xh",)
SIDE_SETS = [[SIDES * z + x for z in planes for x in range(SIDES)] for planes in PLANE_SETS]


def exchange(x, axes, sets):
    return lax.all_to_all(x, axes, 0, 0, tiled=True, axis_index_groups=sets)


def from_partners(x, axes, steps):
    size = lax.axis_size(axes)
    return [lax.ppermute(x, axes, [(i, i ^ step) for i in range(size)]) for step in steps]


def dot_t(a, b):
    return lax.dot_general(a, b, (((1,), (1,)), ((), ())), preferred_element_type=F32)


def pack_kernel(main_heads, guide_heads, qm, km, vm, qg, kg, vg, out_ref):
    for h in range(main_heads + guide_heads):
        at = (h if h < main_heads else h - main_heads) * HD
        for t, ref in enumerate((qm, km, vm) if h < main_heads else (qg, kg, vg)):
            out_ref[h, t] = ref[:, at : at + HD]


def split_two(x):
    high = x.astype(BF16).astype(F32)
    return high, x - high


def attend_kernel(q_ref, kv_ref, map_ref, out_ref, sums_ref):
    rows = out_ref.shape[1]

    def all_pieces(which):
        return kv_ref[:, which].reshape(-1, HD)

    def weighted(queries, shift):
        scores = dot_t(queries, all_pieces(0)) * SCALE
        if shift is not None:
            scores = scores - shift
        values = all_pieces(1)
        values = jnp.concatenate([values, jnp.ones_like(values)], axis=1)
        weights = jnp.exp2(scores).astype(BF16)
        return jnp.dot(weights, values, preferred_element_type=F32)

    def emit(at, total, shift):
        count = total.shape[0]
        lane = lax.broadcasted_iota(jnp.int32, (count, HD), 1)
        picks = lax.broadcasted_iota(jnp.int32, (16, HD), 0) == lax.broadcasted_iota(
            jnp.int32, (16, HD), 1
        )
        out_ref[:CH, at] = dot_t(map_ref[...], total[:, :HD].astype(BF16)).astype(BF16)
        high, low = split_two(total[:, HD:])
        rest = jnp.where(lane == 0, high, jnp.where(lane == 1, low, 0.0))
        if shift is not None:
            high, low = split_two(shift)
            rest = jnp.where(lane == 2, high, jnp.where(lane == 3, low, rest))
        rest = dot_t(picks.astype(F32).astype(BF16), rest.astype(BF16))
        out_ref[CH:, at] = rest.astype(BF16)

    total = weighted(q_ref[...], None)
    emit(slice(None), total, None)
    sums_ref[...] = total[:, HD:]
    least = jnp.min(sums_ref[...])
    most = jnp.max(sums_ref[...])

    @pl.when(jnp.logical_not((least > 1e-20) & (most < 1e25)))
    def _():
        @pl.loop(0, rows // HD)
        def _(i):
            at = pl.ds(pl.multiple_of(i * HD, HD), HD)
            queries = q_ref[at, :]
            top = jnp.max(dot_t(queries, all_pieces(0)), axis=1, keepdims=True)
            shift = jnp.ceil(top * SCALE)
            emit(at, weighted(queries, shift), shift)


def attend(queries, key_values, map_t):
    rows = queries.shape[0]
    keys = key_values.shape[0] * key_values.shape[2]
    return pl.pallas_call(
        attend_kernel,
        in_specs=[VMEM] * 3,
        out_specs=VMEM,
        out_shape=jax.ShapeDtypeStruct((MESSAGE_ROWS, rows), BF16),
        scratch_shapes=[pltpu.VMEM((rows, HD), F32)],
        compiler_params=pltpu.CompilerParams(vmem_limit_bytes=40 << 20),
        cost_estimate=pl.CostEstimate(
            flops=8 * rows * keys * HD, bytes_accessed=2 << 20, transcendentals=rows * keys
        ),
    )(queries, key_values, map_t)


def combine_kernel(gain_ref, *refs):
    *in_refs, out_ref = refs
    half = out_ref.shape[2]
    stats = [ref[CH:, :].astype(F32) for ref in in_refs]
    shifts = [s[2:3] + s[3:4] for s in stats]
    top = functools.reduce(jnp.maximum, shifts)
    scales = [jnp.exp2(shift - top) for shift in shifts]
    summed = sum((s[0:1] + s[1:2]) * scale for s, scale in zip(stats, scales))
    velocity = sum(ref[:CH, :].astype(F32) * scale for ref, scale in zip(in_refs, scales))
    velocity = (velocity * (gain_ref[0] / summed)).T
    velocity = velocity.reshape(out_ref.shape[0], 2, half, CH)
    velocity = jnp.concatenate([velocity[:, 0], velocity[:, 1]], axis=2).astype(BF16)
    for side in range(out_ref.shape[1]):
        out_ref[:, side] = velocity


def body(
    query_main, key_main, value_main, query_guide, key_guide, value_guide, map_main, map_guide
):
    tokens_here = query_main.shape[0]
    main_heads = query_main.shape[1] // HD
    guide_heads = query_guide.shape[1] // HD
    heads = main_heads + guide_heads
    head = lax.axis_index("zh")

    maps = jnp.concatenate([map_main, map_guide], axis=0).reshape(-1, HD, CH)
    map_t = lax.dynamic_index_in_dim(maps, head, 0, keepdims=False).T
    gain = jnp.where(head < main_heads, guidance, 1.0 - guidance).astype(F32).reshape(1)

    with jax.named_scope("pack"):
        packed = pl.pallas_call(
            functools.partial(pack_kernel, main_heads, guide_heads),
            in_specs=[VMEM] * 6,
            out_specs=VMEM,
            out_shape=jax.ShapeDtypeStruct((heads, 3, tokens_here, HD), BF16),
        )(query_main, key_main, value_main, query_guide, key_guide, value_guide)
    with jax.named_scope("to_heads"):
        arrived = exchange(packed, Z, PLANE_SETS)
    with jax.named_scope("gather"):
        kv = arrived[:, 1:]
        copies = jnp.broadcast_to(kv[None], (len(KEY_SETS[0]),) + kv.shape)
        key_values = exchange(copies.reshape((-1,) + kv.shape[1:]), KEY_AXES, KEY_SETS)
        q = arrived[:, 0].reshape(heads * tokens_here, HD)
        queries = from_partners(q, QUERY_AXES, QUERY_STEPS)
    with jax.named_scope("attend"):
        shares = [
            from_partners(attend(piece, key_values, map_t), QUERY_AXES, (step,))[0]
            for piece, step in zip(queries, QUERY_STEPS)
        ]
        shares.append(attend(q, key_values, map_t))
    with jax.named_scope("combine"):
        velocity = pl.pallas_call(
            combine_kernel,
            in_specs=[SMEM] + [VMEM] * len(shares),
            out_specs=VMEM,
            out_shape=jax.ShapeDtypeStruct((heads, SIDES, tokens_here // 2, 2 * CH), BF16),
            compiler_params=SMALL,
        )(gain, *shares)
    with jax.named_scope("to_tokens"):
        velocity = velocity.reshape((heads * SIDES,) + velocity.shape[2:])
        velocity = exchange(velocity, PLANE_AXES, SIDE_SETS)
        velocity = jnp.sum(velocity.astype(F32), axis=0)
        velocity = jnp.sum(lax.all_gather(velocity, "c", axis=0), axis=0)
    return velocity.reshape(tokens_here // 2, 2, CH).transpose(1, 0, 2).reshape(tokens_here, CH)


def solution(mesh):
    fine = Mesh(mesh.devices.reshape(4, 8, 2, 2, 2, 2), SEQ + GRP)
    placed = (P(SEQ, GRP),) * 6 + (P(GRP, None),) * 2
    return jax.shard_map(
        body, mesh=fine, in_specs=placed, out_specs=P(SEQ, None), check_vma=False
    )
```

```python
import functools
import math

import jax
import jax.numpy as jnp
from jax import lax
from jax.experimental import pallas as pl
from jax.experimental.pallas import tpu as pltpu
from jax.sharding import Mesh
from jax.sharding import PartitionSpec as P

HD = 128
CH = 64
guidance = 2.5
SCALE = math.log2(math.e) / math.sqrt(HD)
F32 = jnp.float32
BF16 = jnp.bfloat16
VMEM = pl.BlockSpec(memory_space=pltpu.VMEM)
SMEM = pl.BlockSpec(memory_space=pltpu.SMEM)
SMALL = pltpu.CompilerParams(vmem_limit_bytes=12 << 20)
MESSAGE_ROWS = CH + 16

SEQ = ("y", "zh", "z0", "xl")
GRP = ("xh", "c")
Z = ("zh", "z0")
PLANE_SETS = ([0, 2, 4, 6, 9, 11, 13, 15], [1, 3, 5, 7, 8, 10, 12, 14])
FIRST = (0, 1, 6, 7)
SECOND = (4, 5, 2, 3)
QUERY_ORDER = SECOND + FIRST
QUERY_AXES = ("y", "z0")
QUERY_STEPS = (1, 6, 7)
KEY_AXES = ("y", "xl")
KEY_SETS = ([0, 1, 2, 3], [4, 5, 6, 7])
SIDES = 2
PLANE_AXES = Z + ("xh",)
SIDE_SETS = [[SIDES * z + x for z in planes for x in range(SIDES)] for planes in PLANE_SETS]


def exchange(x, axes, sets):
    return lax.all_to_all(x, axes, 0, 0, tiled=True, axis_index_groups=sets)


def from_place(x, step):
    pairs = [(planes[i], planes[i ^ step]) for planes in PLANE_SETS for i in range(len(planes))]
    return lax.ppermute(x, Z, pairs)


def from_partners(x, axes, steps):
    size = lax.axis_size(axes)
    return [lax.ppermute(x, axes, [(i, i ^ step) for i in range(size)]) for step in steps]


def dot_t(a, b):
    return lax.dot_general(a, b, (((1,), (1,)), ((), ())), preferred_element_type=F32)


def pack_kernel(main_heads, guide_heads, place_ref, qm, km, vm, qg, kg, vg, *out_refs):
    heads = main_heads + guide_heads
    for place in range(heads):

        @pl.when(place_ref[0] == place)
        def _():
            for j, out_ref in enumerate(out_refs):
                h = place ^ j
                at = (h if h < main_heads else h - main_heads) * HD
                for t, ref in enumerate((qm, km, vm) if h < main_heads else (qg, kg, vg)):
                    out_ref[t] = ref[:, at : at + HD]


def join_kernel(pieces, with_queries, *refs):
    in_refs, (copies_ref, *rest) = refs[:pieces], refs[pieces:]
    for copy in range(copies_ref.shape[0]):
        for i in range(copies_ref.shape[1]):
            copies_ref[copy, i] = in_refs[i][1:]
    if with_queries:
        (q_ref,) = rest
        step = in_refs[0].shape[1]
        for i, j in enumerate(QUERY_ORDER):
            q_ref[j * step : (j + 1) * step, :] = in_refs[i][0]


def join(pieces, keys_of, with_queries):
    _, tokens, _ = pieces[0].shape
    shapes = [jax.ShapeDtypeStruct((len(KEY_SETS[0]), keys_of, 2, tokens, HD), BF16)]
    if with_queries:
        shapes.append(jax.ShapeDtypeStruct((len(pieces) * tokens, HD), BF16))
    copies, *rest = pl.pallas_call(
        functools.partial(join_kernel, len(pieces), with_queries),
        in_specs=[VMEM] * len(pieces),
        out_specs=[VMEM] * len(shapes),
        out_shape=shapes,
        compiler_params=SMALL,
    )(*pieces)
    return copies.reshape((-1,) + copies.shape[2:]), *rest


def split_two(x):
    high = x.astype(BF16).astype(F32)
    return high, x - high


def attend_kernel(q_ref, *refs):
    *kv_refs, map_ref, out_ref, sums_ref = refs
    rows = out_ref.shape[1]

    def all_pieces(which):
        return jnp.concatenate([ref[:, which].reshape(-1, HD) for ref in kv_refs], axis=0)

    def weighted(queries, shift):
        scores = dot_t(queries, all_pieces(0)) * SCALE
        if shift is not None:
            scores = scores - shift
        values = all_pieces(1)
        values = jnp.concatenate([values, jnp.ones_like(values)], axis=1)
        weights = jnp.exp2(scores).astype(BF16)
        return jnp.dot(weights, values, preferred_element_type=F32)

    def emit(at, total, shift):
        count = total.shape[0]
        lane = lax.broadcasted_iota(jnp.int32, (count, HD), 1)
        picks = lax.broadcasted_iota(jnp.int32, (16, HD), 0) == lax.broadcasted_iota(
            jnp.int32, (16, HD), 1
        )
        out_ref[:CH, at] = dot_t(map_ref[...], total[:, :HD].astype(BF16)).astype(BF16)
        high, low = split_two(total[:, HD:])
        rest = jnp.where(lane == 0, high, jnp.where(lane == 1, low, 0.0))
        if shift is not None:
            high, low = split_two(shift)
            rest = jnp.where(lane == 2, high, jnp.where(lane == 3, low, rest))
        rest = dot_t(picks.astype(F32).astype(BF16), rest.astype(BF16))
        out_ref[CH:, at] = rest.astype(BF16)

    total = weighted(q_ref[...], None)
    emit(slice(None), total, None)
    sums_ref[...] = total[:, HD:]
    least = jnp.min(sums_ref[...])
    most = jnp.max(sums_ref[...])

    @pl.when(jnp.logical_not((least > 1e-20) & (most < 1e25)))
    def _():
        @pl.loop(0, rows // HD)
        def _(i):
            at = pl.ds(pl.multiple_of(i * HD, HD), HD)
            queries = q_ref[at, :]
            top = jnp.max(dot_t(queries, all_pieces(0)), axis=1, keepdims=True)
            shift = jnp.ceil(top * SCALE)
            emit(at, weighted(queries, shift), shift)


def attend(queries, key_values, map_t):
    rows = queries.shape[0]
    keys = key_values[0].shape[0] * key_values[0].shape[2] * len(key_values)
    return pl.pallas_call(
        attend_kernel,
        in_specs=[VMEM] * (2 + len(key_values)),
        out_specs=VMEM,
        out_shape=jax.ShapeDtypeStruct((MESSAGE_ROWS, rows), BF16),
        scratch_shapes=[pltpu.VMEM((rows, HD), F32)],
        compiler_params=pltpu.CompilerParams(vmem_limit_bytes=40 << 20),
        cost_estimate=pl.CostEstimate(
            flops=8 * rows * keys * HD, bytes_accessed=2 << 20, transcendentals=rows * keys
        ),
    )(queries, *key_values, map_t)


def combine_kernel(place_ref, gain_ref, *refs):
    *in_refs, out_ref = refs
    half = out_ref.shape[2]
    stats = [ref[CH:, :].astype(F32) for ref in in_refs]
    shifts = [s[2:3] + s[3:4] for s in stats]
    top = functools.reduce(jnp.maximum, shifts)
    scales = [jnp.exp2(shift - top) for shift in shifts]
    summed = sum((s[0:1] + s[1:2]) * scale for s, scale in zip(stats, scales))
    velocity = sum(ref[:CH, :].astype(F32) * scale for ref, scale in zip(in_refs, scales))
    velocity = (velocity * (gain_ref[0] / summed)).T
    velocity = velocity.reshape(out_ref.shape[0], 2, half, CH)
    velocity = jnp.concatenate([velocity[:, 0], velocity[:, 1]], axis=2).astype(BF16)
    for j in range(out_ref.shape[0]):
        for side in range(out_ref.shape[1]):
            out_ref[place_ref[0] ^ j, side] = velocity[j]


def body(
    query_main, key_main, value_main, query_guide, key_guide, value_guide, map_main, map_guide
):
    tokens_here = query_main.shape[0]
    main_heads = query_main.shape[1] // HD
    guide_heads = query_guide.shape[1] // HD
    heads = main_heads + guide_heads
    head = lax.axis_index("zh")

    maps = jnp.concatenate([map_main, map_guide], axis=0).reshape(-1, HD, CH)
    map_t = lax.dynamic_index_in_dim(maps, head, 0, keepdims=False).T
    gain = jnp.where(head < main_heads, guidance, 1.0 - guidance).astype(F32).reshape(1)

    place = head.astype(jnp.int32).reshape(1)
    with jax.named_scope("pack"):
        packed = pl.pallas_call(
            functools.partial(pack_kernel, main_heads, guide_heads),
            in_specs=[SMEM] + [VMEM] * 6,
            out_specs=[VMEM] * heads,
            out_shape=[jax.ShapeDtypeStruct((3, tokens_here, HD), BF16)] * heads,
        )(place, query_main, key_main, value_main, query_guide, key_guide, value_guide)
    with jax.named_scope("to_heads"):
        first = [from_place(packed[j], j) if j else packed[j] for j in FIRST]
        second = [from_place(packed[j], j) for j in SECOND]
    with jax.named_scope("gather"):
        (copies,) = join(first, len(FIRST), False)
        key_values = [exchange(copies, KEY_AXES, KEY_SETS)]
        key_values[0], second = lax.optimization_barrier((key_values[0], second))
        copies, q = join(second + first, len(SECOND), True)
        key_values.append(exchange(copies, KEY_AXES, KEY_SETS))
        queries = from_partners(q, QUERY_AXES, QUERY_STEPS)
    with jax.named_scope("attend"):
        shares = [
            from_partners(attend(piece, key_values, map_t), QUERY_AXES, (step,))[0]
            for piece, step in zip(queries, QUERY_STEPS)
        ]
        shares.append(attend(q, key_values, map_t))
    with jax.named_scope("combine"):
        velocity = pl.pallas_call(
            combine_kernel,
            in_specs=[SMEM] * 2 + [VMEM] * len(shares),
            out_specs=VMEM,
            out_shape=jax.ShapeDtypeStruct((heads, SIDES, tokens_here // 2, 2 * CH), BF16),
            compiler_params=SMALL,
        )(place, gain, *shares)
    with jax.named_scope("to_tokens"):
        velocity = velocity.reshape((heads * SIDES,) + velocity.shape[2:])
        velocity = exchange(velocity, PLANE_AXES, SIDE_SETS)
        velocity = jnp.sum(velocity.astype(F32), axis=0)
        velocity = jnp.sum(lax.all_gather(velocity, "c", axis=0), axis=0)
    return velocity.reshape(tokens_here // 2, 2, CH).transpose(1, 0, 2).reshape(tokens_here, CH)


def solution(mesh):
    fine = Mesh(mesh.devices.reshape(4, 8, 2, 2, 2, 2), SEQ + GRP)
    placed = (P(SEQ, GRP),) * 6 + (P(GRP, None),) * 2
    return jax.shard_map(
        body, mesh=fine, in_specs=placed, out_specs=P(SEQ, None), check_vma=False
    )
```

```python
import functools
import math

import jax
import jax.numpy as jnp
from jax import lax
from jax.experimental import pallas as pl
from jax.experimental.pallas import tpu as pltpu
from jax.sharding import Mesh
from jax.sharding import PartitionSpec as P

HD = 128
CH = 64
guidance = 2.5
SCALE = math.log2(math.e) / math.sqrt(HD)
F32 = jnp.float32
BF16 = jnp.bfloat16
VMEM = pl.BlockSpec(memory_space=pltpu.VMEM)
SMEM = pl.BlockSpec(memory_space=pltpu.SMEM)
SMALL = pltpu.CompilerParams(vmem_limit_bytes=12 << 20)
MESSAGE_ROWS = CH + 16

SEQ = ("y", "zh", "z0", "xl")
GRP = ("xh", "c")
Z = ("zh", "z0")
PLANE_SETS = ([0, 2, 4, 6, 9, 11, 13, 15], [1, 3, 5, 7, 8, 10, 12, 14])
QUERY_AXES = ("y", "z0")
QUERY_STEPS = (1, 6, 7)
QUERY_SETS = ([0, 1, 6, 7], [2, 3, 4, 5])
KEY_AXES = ("y", "xl")
KEY_SETS = ([0, 1, 2, 3], [4, 5, 6, 7])
SIDES = 2
PLANE_AXES = Z + ("xh",)
SIDE_SETS = [[SIDES * z + x for z in planes for x in range(SIDES)] for planes in PLANE_SETS]


def exchange(x, axes, sets):
    return lax.all_to_all(x, axes, 0, 0, tiled=True, axis_index_groups=sets)


def from_partners(x, axes, steps):
    size = lax.axis_size(axes)
    return [lax.ppermute(x, axes, [(i, i ^ step) for i in range(size)]) for step in steps]


def dot_t(a, b):
    return lax.dot_general(a, b, (((1,), (1,)), ((), ())), preferred_element_type=F32)


def pack_kernel(main_heads, guide_heads, qm, km, vm, qg, kg, vg, out_ref):
    for h in range(main_heads + guide_heads):
        at = (h if h < main_heads else h - main_heads) * HD
        for t, ref in enumerate((qm, km, vm) if h < main_heads else (qg, kg, vg)):
            out_ref[h, t] = ref[:, at : at + HD]


def copy_kernel(in_ref, q_ref, copies_ref):
    heads, _, tokens, _ = in_ref.shape
    for h in range(heads):
        q_ref[h * tokens : (h + 1) * tokens, :] = in_ref[h, 0]
        for copy in range(copies_ref.shape[0]):
            copies_ref[copy, h] = in_ref[h, 1:]


def split_two(x):
    high = x.astype(BF16).astype(F32)
    return high, x - high


def attend_kernel(place_ref, *refs):
    *q_refs, kv_ref, map_ref, out_ref, sums_ref = refs
    rows = out_ref.shape[2]

    def all_pieces(which):
        return kv_ref[:, which].reshape(-1, HD)

    def weighted(queries, shift):
        scores = dot_t(queries, all_pieces(0)) * SCALE
        if shift is not None:
            scores = scores - shift
        values = all_pieces(1)
        values = jnp.concatenate([values, jnp.ones_like(values)], axis=1)
        weights = jnp.exp2(scores).astype(BF16)
        return jnp.dot(weights, values, preferred_element_type=F32)

    def emit(k, at, total, shift):
        to = place_ref[0] ^ k
        count = total.shape[0]
        lane = lax.broadcasted_iota(jnp.int32, (count, HD), 1)
        picks = lax.broadcasted_iota(jnp.int32, (16, HD), 0) == lax.broadcasted_iota(
            jnp.int32, (16, HD), 1
        )
        out_ref[to, :CH, at] = dot_t(map_ref[...], total[:, :HD].astype(BF16)).astype(BF16)
        high, low = split_two(total[:, HD:])
        rest = jnp.where(lane == 0, high, jnp.where(lane == 1, low, 0.0))
        if shift is not None:
            high, low = split_two(shift)
            rest = jnp.where(lane == 2, high, jnp.where(lane == 3, low, rest))
        rest = dot_t(picks.astype(F32).astype(BF16), rest.astype(BF16))
        out_ref[to, CH:, at] = rest.astype(BF16)

    for k, q_ref in enumerate(q_refs):
        total = weighted(q_ref[...], None)
        emit(k, slice(None), total, None)
        sums_ref[k] = total[:, HD:]

    for k, q_ref in enumerate(q_refs):
        least = jnp.min(sums_ref[k])
        most = jnp.max(sums_ref[k])

        @pl.when(jnp.logical_not((least > 1e-20) & (most < 1e25)))
        def _():
            @pl.loop(0, rows // HD)
            def _(i):
                at = pl.ds(pl.multiple_of(i * HD, HD), HD)
                queries = q_ref[at, :]
                top = jnp.max(dot_t(queries, all_pieces(0)), axis=1, keepdims=True)
                shift = jnp.ceil(top * SCALE)
                emit(k, at, weighted(queries, shift), shift)


def attend(place, queries, key_values, map_t):
    rows = queries[0].shape[0]
    keys = key_values.shape[0] * key_values.shape[2]
    blocks = len(queries)
    return pl.pallas_call(
        attend_kernel,
        in_specs=[SMEM] + [VMEM] * (2 + blocks),
        out_specs=VMEM,
        out_shape=jax.ShapeDtypeStruct((blocks, MESSAGE_ROWS, rows), BF16),
        scratch_shapes=[pltpu.VMEM((blocks, rows, HD), F32)],
        compiler_params=pltpu.CompilerParams(vmem_limit_bytes=48 << 20),
        cost_estimate=pl.CostEstimate(
            flops=8 * blocks * rows * keys * HD,
            bytes_accessed=2 << 20,
            transcendentals=blocks * rows * keys,
        ),
    )(place, *queries, key_values, map_t)


def combine_kernel(gain_ref, in_ref, out_ref):
    in_refs = [in_ref.at[k] for k in range(in_ref.shape[0])]
    half = out_ref.shape[2]
    stats = [ref[CH:, :].astype(F32) for ref in in_refs]
    shifts = [s[2:3] + s[3:4] for s in stats]
    top = functools.reduce(jnp.maximum, shifts)
    scales = [jnp.exp2(shift - top) for shift in shifts]
    summed = sum((s[0:1] + s[1:2]) * scale for s, scale in zip(stats, scales))
    velocity = sum(ref[:CH, :].astype(F32) * scale for ref, scale in zip(in_refs, scales))
    velocity = (velocity * (gain_ref[0] / summed)).T
    velocity = velocity.reshape(out_ref.shape[0], 2, half, CH)
    velocity = jnp.concatenate([velocity[:, 0], velocity[:, 1]], axis=2).astype(BF16)
    for side in range(out_ref.shape[1]):
        out_ref[:, side] = velocity


def body(
    query_main, key_main, value_main, query_guide, key_guide, value_guide, map_main, map_guide
):
    tokens_here = query_main.shape[0]
    main_heads = query_main.shape[1] // HD
    guide_heads = query_guide.shape[1] // HD
    heads = main_heads + guide_heads
    head = lax.axis_index("zh")

    maps = jnp.concatenate([map_main, map_guide], axis=0).reshape(-1, HD, CH)
    map_t = lax.dynamic_index_in_dim(maps, head, 0, keepdims=False).T
    gain = jnp.where(head < main_heads, guidance, 1.0 - guidance).astype(F32).reshape(1)

    with jax.named_scope("pack"):
        packed = pl.pallas_call(
            functools.partial(pack_kernel, main_heads, guide_heads),
            in_specs=[VMEM] * 6,
            out_specs=VMEM,
            out_shape=jax.ShapeDtypeStruct((heads, 3, tokens_here, HD), BF16),
        )(query_main, key_main, value_main, query_guide, key_guide, value_guide)
    with jax.named_scope("to_heads"):
        arrived = exchange(packed, Z, PLANE_SETS)
    with jax.named_scope("gather"):
        copies = (len(KEY_SETS[0]), heads, 2, tokens_here, HD)
        q, copies = pl.pallas_call(
            copy_kernel,
            in_specs=[VMEM],
            out_specs=[VMEM] * 2,
            out_shape=[
                jax.ShapeDtypeStruct((heads * tokens_here, HD), BF16),
                jax.ShapeDtypeStruct(copies, BF16),
            ],
            compiler_params=SMALL,
        )(arrived)
        key_values = exchange(copies.reshape((-1,) + copies.shape[2:]), KEY_AXES, KEY_SETS)
        queries = [q] + from_partners(q, QUERY_AXES, QUERY_STEPS)
    with jax.named_scope("attend"):
        place = (lax.axis_index("y") >> 1) * 2 + lax.axis_index("z0")
        shares = attend(place.astype(jnp.int32).reshape(1), queries, key_values, map_t)
    with jax.named_scope("combine"):
        shares = exchange(shares, QUERY_AXES, QUERY_SETS)
        velocity = pl.pallas_call(
            combine_kernel,
            in_specs=[SMEM, VMEM],
            out_specs=VMEM,
            out_shape=jax.ShapeDtypeStruct((heads, SIDES, tokens_here // 2, 2 * CH), BF16),
            compiler_params=SMALL,
        )(gain, shares)
    with jax.named_scope("to_tokens"):
        velocity = velocity.reshape((heads * SIDES,) + velocity.shape[2:])
        velocity = exchange(velocity, PLANE_AXES, SIDE_SETS)
        velocity = jnp.sum(velocity.astype(F32), axis=0)
        velocity = jnp.sum(lax.all_gather(velocity, "c", axis=0), axis=0)
    return velocity.reshape(tokens_here // 2, 2, CH).transpose(1, 0, 2).reshape(tokens_here, CH)


def solution(mesh):
    fine = Mesh(mesh.devices.reshape(4, 8, 2, 2, 2, 2), SEQ + GRP)
    placed = (P(SEQ, GRP),) * 6 + (P(GRP, None),) * 2
    return jax.shard_map(
        body, mesh=fine, in_specs=placed, out_specs=P(SEQ, None), check_vma=False
    )
```

```python
import functools
import math

import jax
import jax.numpy as jnp
from jax import lax
from jax.experimental import pallas as pl
from jax.experimental.pallas import tpu as pltpu
from jax.sharding import Mesh
from jax.sharding import PartitionSpec as P

HD = 128
CH = 64
guidance = 2.5
SCALE = math.log2(math.e) / math.sqrt(HD)
F32 = jnp.float32
BF16 = jnp.bfloat16
VMEM = pl.BlockSpec(memory_space=pltpu.VMEM)
SMEM = pl.BlockSpec(memory_space=pltpu.SMEM)
SMALL = pltpu.CompilerParams(vmem_limit_bytes=12 << 20)
MESSAGE_ROWS = CH + 16

SEQ = ("y", "zh", "z0", "xl")
GRP = ("xh", "c")
Z = ("zh", "z0")
PLANE_SETS = ([0, 2, 4, 6, 9, 11, 13, 15], [1, 3, 5, 7, 8, 10, 12, 14])
QUERY_AXES = ("y", "z0")
Z0_STEP, Y_STEP = 1, 6
KEY_AXES = ("y", "xl")
KEY_SETS = ([0, 1, 2, 3], [4, 5, 6, 7])
SIDES = 2
PLANE_AXES = Z + ("xh",)
SIDE_SETS = [[SIDES * z + x for z in planes for x in range(SIDES)] for planes in PLANE_SETS]


def exchange(x, axes, sets):
    return lax.all_to_all(x, axes, 0, 0, tiled=True, axis_index_groups=sets)


def from_partner(x, step):
    size = lax.axis_size(QUERY_AXES)
    return lax.ppermute(x, QUERY_AXES, [(i, i ^ step) for i in range(size)])


def dot_t(a, b):
    return lax.dot_general(a, b, (((1,), (1,)), ((), ())), preferred_element_type=F32)


def pack_kernel(main_heads, guide_heads, qm, km, vm, qg, kg, vg, out_ref):
    for h in range(main_heads + guide_heads):
        at = (h if h < main_heads else h - main_heads) * HD
        for t, ref in enumerate((qm, km, vm) if h < main_heads else (qg, kg, vg)):
            out_ref[h, t] = ref[:, at : at + HD]


def copy_kernel(in_ref, q_ref, copies_ref):
    heads, _, tokens, _ = in_ref.shape
    for h in range(heads):
        q_ref[h * tokens : (h + 1) * tokens, :] = in_ref[h, 0]
        for copy in range(copies_ref.shape[0]):
            copies_ref[copy, h] = in_ref[h, 1:]


def split_two(x):
    high = x.astype(BF16).astype(F32)
    return high, x - high


def attend_kernel(*refs):
    *q_refs, kv_ref, map_ref, out_ref, staged_ref, sums_ref = refs
    rows = out_ref.shape[2]
    for k, q_ref in enumerate(q_refs):
        staged_ref[k] = q_ref[...]

    def all_pieces(which):
        return kv_ref[:, which].reshape(-1, HD)

    def weighted(queries, shift):
        scores = dot_t(queries, all_pieces(0)) * SCALE
        if shift is not None:
            scores = scores - shift
        values = all_pieces(1)
        values = jnp.concatenate([values, jnp.ones_like(values)], axis=1)
        weights = jnp.exp2(scores).astype(BF16)
        return jnp.dot(weights, values, preferred_element_type=F32)

    def emit(k, at, total, shift):
        count = total.shape[0]
        lane = lax.broadcasted_iota(jnp.int32, (count, HD), 1)
        picks = lax.broadcasted_iota(jnp.int32, (16, HD), 0) == lax.broadcasted_iota(
            jnp.int32, (16, HD), 1
        )
        out_ref[k, :CH, at] = dot_t(map_ref[...], total[:, :HD].astype(BF16)).astype(BF16)
        high, low = split_two(total[:, HD:])
        rest = jnp.where(lane == 0, high, jnp.where(lane == 1, low, 0.0))
        if shift is not None:
            high, low = split_two(shift)
            rest = jnp.where(lane == 2, high, jnp.where(lane == 3, low, rest))
        rest = dot_t(picks.astype(F32).astype(BF16), rest.astype(BF16))
        out_ref[k, CH:, at] = rest.astype(BF16)

    @pl.loop(0, len(q_refs))
    def _(k):
        total = weighted(staged_ref[k], None)
        emit(k, slice(None), total, None)
        sums_ref[...] = total[:, HD:]
        least = jnp.min(sums_ref[...])
        most = jnp.max(sums_ref[...])

        @pl.when(jnp.logical_not((least > 1e-20) & (most < 1e25)))
        def _():
            @pl.loop(0, rows // HD)
            def _(i):
                at = pl.ds(pl.multiple_of(i * HD, HD), HD)
                queries = staged_ref[k, at, :]
                top = jnp.max(dot_t(queries, all_pieces(0)), axis=1, keepdims=True)
                shift = jnp.ceil(top * SCALE)
                emit(k, at, weighted(queries, shift), shift)


def attend(queries, key_values, map_t):
    rows = queries[0].shape[0]
    keys = key_values.shape[0] * key_values.shape[2]
    blocks = len(queries)
    return pl.pallas_call(
        attend_kernel,
        in_specs=[VMEM] * (2 + blocks),
        out_specs=VMEM,
        out_shape=jax.ShapeDtypeStruct((blocks, MESSAGE_ROWS, rows), BF16),
        scratch_shapes=[pltpu.VMEM((blocks, rows, HD), BF16), pltpu.VMEM((rows, HD), F32)],
        compiler_params=pltpu.CompilerParams(vmem_limit_bytes=40 << 20),
        cost_estimate=pl.CostEstimate(
            flops=8 * blocks * rows * keys * HD,
            bytes_accessed=2 << 20,
            transcendentals=blocks * rows * keys,
        ),
    )(*queries, key_values, map_t)


def added(shares):
    stats = [share[CH:, :].astype(F32) for share in shares]
    shifts = [s[2:3] + s[3:4] for s in stats]
    top = functools.reduce(jnp.maximum, shifts)
    scales = [jnp.exp2(shift - top) for shift in shifts]
    summed = sum((s[0:1] + s[1:2]) * scale for s, scale in zip(stats, scales))
    velocity = sum(share[:CH, :].astype(F32) * scale for share, scale in zip(shares, scales))
    return velocity, summed, top


def add_kernel(here_ref, there_ref, out_ref):
    velocity, summed, top = added([here_ref[1], there_ref[1]])
    out_ref[:CH, :] = velocity.astype(BF16)
    tail = split_two(summed) + split_two(top)
    filler = jnp.zeros((out_ref.shape[0] - CH - len(tail), out_ref.shape[1]), F32)
    out_ref[CH:, :] = jnp.concatenate(tail + (filler,), axis=0).astype(BF16)


def combine_kernel(gain_ref, here_ref, there_ref, beside_ref, out_ref):
    half = out_ref.shape[2]
    velocity, summed, _ = added([here_ref[0], there_ref[0], beside_ref[...]])
    velocity = (velocity * (gain_ref[0] / summed)).T
    velocity = velocity.reshape(out_ref.shape[0], 2, half, CH)
    velocity = jnp.concatenate([velocity[:, 0], velocity[:, 1]], axis=2).astype(BF16)
    for side in range(out_ref.shape[1]):
        out_ref[:, side] = velocity


def body(
    query_main, key_main, value_main, query_guide, key_guide, value_guide, map_main, map_guide
):
    tokens_here = query_main.shape[0]
    main_heads = query_main.shape[1] // HD
    guide_heads = query_guide.shape[1] // HD
    heads = main_heads + guide_heads
    head = lax.axis_index("zh")

    maps = jnp.concatenate([map_main, map_guide], axis=0).reshape(-1, HD, CH)
    map_t = lax.dynamic_index_in_dim(maps, head, 0, keepdims=False).T
    gain = jnp.where(head < main_heads, guidance, 1.0 - guidance).astype(F32).reshape(1)

    with jax.named_scope("pack"):
        packed = pl.pallas_call(
            functools.partial(pack_kernel, main_heads, guide_heads),
            in_specs=[VMEM] * 6,
            out_specs=VMEM,
            out_shape=jax.ShapeDtypeStruct((heads, 3, tokens_here, HD), BF16),
        )(query_main, key_main, value_main, query_guide, key_guide, value_guide)
    with jax.named_scope("to_heads"):
        arrived = exchange(packed, Z, PLANE_SETS)
    with jax.named_scope("gather"):
        copies = (len(KEY_SETS[0]), heads, 2, tokens_here, HD)
        q, copies = pl.pallas_call(
            copy_kernel,
            in_specs=[VMEM],
            out_specs=[VMEM] * 2,
            out_shape=[
                jax.ShapeDtypeStruct((heads * tokens_here, HD), BF16),
                jax.ShapeDtypeStruct(copies, BF16),
            ],
            compiler_params=SMALL,
        )(arrived)
        key_values = exchange(copies.reshape((-1,) + copies.shape[2:]), KEY_AXES, KEY_SETS)
        beside = from_partner(q, Z0_STEP)
        across = [from_partner(q, Y_STEP), from_partner(q, Y_STEP ^ Z0_STEP)]
    with jax.named_scope("attend"):
        there = from_partner(attend(across, key_values, map_t), Y_STEP)
        here = attend([q, beside], key_values, map_t)
    with jax.named_scope("combine"):
        share = pl.pallas_call(
            add_kernel,
            in_specs=[VMEM] * 2,
            out_specs=VMEM,
            out_shape=jax.ShapeDtypeStruct(here.shape[1:], BF16),
            compiler_params=SMALL,
        )(here, there)
        velocity = pl.pallas_call(
            combine_kernel,
            in_specs=[SMEM] + [VMEM] * 3,
            out_specs=VMEM,
            out_shape=jax.ShapeDtypeStruct((heads, SIDES, tokens_here // 2, 2 * CH), BF16),
            compiler_params=SMALL,
        )(gain, here, there, from_partner(share, Z0_STEP))
    with jax.named_scope("to_tokens"):
        velocity = velocity.reshape((heads * SIDES,) + velocity.shape[2:])
        velocity = exchange(velocity, PLANE_AXES, SIDE_SETS)
        velocity = jnp.sum(velocity.astype(F32), axis=0)
        velocity = jnp.sum(lax.all_gather(velocity, "c", axis=0), axis=0)
    return velocity.reshape(tokens_here // 2, 2, CH).transpose(1, 0, 2).reshape(tokens_here, CH)


def solution(mesh):
    fine = Mesh(mesh.devices.reshape(4, 8, 2, 2, 2, 2), SEQ + GRP)
    placed = (P(SEQ, GRP),) * 6 + (P(GRP, None),) * 2
    return jax.shard_map(
        body, mesh=fine, in_specs=placed, out_specs=P(SEQ, None), check_vma=False
    )
```

```python
import functools
import math

import jax
import jax.numpy as jnp
from jax import lax
from jax.experimental import pallas as pl
from jax.experimental.pallas import tpu as pltpu
from jax.sharding import Mesh
from jax.sharding import PartitionSpec as P

HD = 128
CH = 64
guidance = 2.5
SCALE = math.log2(math.e) / math.sqrt(HD)
F32 = jnp.float32
BF16 = jnp.bfloat16
VMEM = pl.BlockSpec(memory_space=pltpu.VMEM)
SMEM = pl.BlockSpec(memory_space=pltpu.SMEM)
SMALL = pltpu.CompilerParams(vmem_limit_bytes=12 << 20)
MESSAGE_ROWS = CH + 16

SEQ = ("y", "zh", "z0", "xl")
GRP = ("xh", "c")
Z = ("zh", "z0")
PLANE_SETS = ([0, 2, 4, 6, 9, 11, 13, 15], [1, 3, 5, 7, 8, 10, 12, 14])
QUERY_AXES = ("y", "z0")
Z0_STEP, Y_STEP = 1, 6
KEY_AXES = ("y", "xl")
NEAR_STEPS, FAR_STEP = (1, 2), 3
SIDES = 2
PLANE_AXES = Z + ("xh",)
SIDE_SETS = [[SIDES * z + x for z in planes for x in range(SIDES)] for planes in PLANE_SETS]


def exchange(x, axes, sets):
    return lax.all_to_all(x, axes, 0, 0, tiled=True, axis_index_groups=sets)


def from_partner(x, step, axes=QUERY_AXES):
    return lax.ppermute(x, axes, [(i, i ^ step) for i in range(lax.axis_size(axes))])


def dot_t(a, b):
    return lax.dot_general(a, b, (((1,), (1,)), ((), ())), preferred_element_type=F32)


def pack_kernel(main_heads, guide_heads, qm, km, vm, qg, kg, vg, out_ref):
    for h in range(main_heads + guide_heads):
        at = (h if h < main_heads else h - main_heads) * HD
        for t, ref in enumerate((qm, km, vm) if h < main_heads else (qg, kg, vg)):
            out_ref[h, t] = ref[:, at : at + HD]


def copy_kernel(in_ref, q_ref, kv_ref):
    heads, _, tokens, _ = in_ref.shape
    for h in range(heads):
        q_ref[h * tokens : (h + 1) * tokens, :] = in_ref[h, 0]
        kv_ref[h] = in_ref[h, 1:]


def split_two(x):
    high = x.astype(BF16).astype(F32)
    return high, x - high


def message(velocity, summed, top, rows, dtype):
    tail = split_two(summed) + split_two(top) if dtype == BF16 else (summed, top)
    filler = jnp.zeros((rows - CH - len(tail), velocity.shape[1]), F32)
    return jnp.concatenate((velocity,) + tail + (filler,), axis=0).astype(dtype)


def attend_kernel(count, pieces, first_before, *refs):
    q_refs, kv_refs, map_ref, refs = refs[:count], refs[count:pieces], refs[pieces], refs[pieces + 1 :]
    before_ref, refs = (None, refs) if first_before is None else (refs[0], refs[1:])
    out_ref, staged_ref, sums_ref = refs
    rows = out_ref.shape[2]
    for k, q_ref in enumerate(q_refs):
        staged_ref[k] = q_ref[...]

    def all_pieces(which):
        return jnp.concatenate([ref[:, which].reshape(-1, HD) for ref in kv_refs], axis=0)

    def weighted(queries, shift):
        scores = dot_t(queries, all_pieces(0)) * SCALE
        if shift is not None:
            scores = scores - shift
        values = all_pieces(1)
        values = jnp.concatenate([values, jnp.ones_like(values)], axis=1)
        weights = jnp.exp2(scores).astype(BF16)
        return jnp.dot(weights, values, preferred_element_type=F32)

    def emit(k, at, total, shift):
        count = total.shape[0]
        lane = lax.broadcasted_iota(jnp.int32, (count, HD), 1)
        picks = lax.broadcasted_iota(jnp.int32, (16, HD), 0) == lax.broadcasted_iota(
            jnp.int32, (16, HD), 1
        )
        velocity = dot_t(map_ref[...], total[:, :HD].astype(BF16))
        high, low = split_two(total[:, HD:])
        rest = jnp.where(lane == 0, high, jnp.where(lane == 1, low, 0.0))
        if shift is not None:
            high, low = split_two(shift)
            rest = jnp.where(lane == 2, high, jnp.where(lane == 3, low, rest))
        rest = dot_t(picks.astype(F32).astype(BF16), rest.astype(BF16))
        summed, top = rest[0:1] + rest[1:2], rest[2:3] + rest[3:4]
        if before_ref is not None:
            before = before_ref[first_before + k, :, at]
            velocity, summed, top = joined(
                [velocity, before[:CH]], [summed, before[CH : CH + 1]], [top, before[CH + 1 : CH + 2]]
            )
        out_ref[k, :, at] = message(velocity, summed, top, out_ref.shape[1], out_ref.dtype)

    @pl.loop(0, len(q_refs))
    def _(k):
        total = weighted(staged_ref[k], None)
        emit(k, slice(None), total, None)
        sums_ref[...] = total[:, HD:]
        least = jnp.min(sums_ref[...])
        most = jnp.max(sums_ref[...])

        @pl.when(jnp.logical_not((least > 1e-20) & (most < 1e25)))
        def _():
            @pl.loop(0, rows // HD)
            def _(i):
                at = pl.ds(pl.multiple_of(i * HD, HD), HD)
                queries = staged_ref[k, at, :]
                top = jnp.max(dot_t(queries, all_pieces(0)), axis=1, keepdims=True)
                shift = jnp.ceil(top * SCALE)
                emit(k, at, weighted(queries, shift), shift)


def attend(queries, key_values, map_t, before=None, first_before=None):
    rows = queries[0].shape[0]
    keys = key_values[0].shape[0] * key_values[0].shape[2] * len(key_values)
    blocks = len(queries)
    pieces = blocks + len(key_values)
    operands = [*queries, *key_values, map_t] + ([] if before is None else [before])
    out = (blocks, CH + 8, rows) if before is None else (blocks, MESSAGE_ROWS, rows)
    return pl.pallas_call(
        functools.partial(attend_kernel, blocks, pieces, first_before),
        in_specs=[VMEM] * len(operands),
        out_specs=VMEM,
        out_shape=jax.ShapeDtypeStruct(out, F32 if before is None else BF16),
        scratch_shapes=[pltpu.VMEM((blocks, rows, HD), BF16), pltpu.VMEM((rows, HD), F32)],
        compiler_params=pltpu.CompilerParams(vmem_limit_bytes=40 << 20),
        cost_estimate=pl.CostEstimate(
            flops=8 * blocks * rows * keys * HD,
            bytes_accessed=2 << 20,
            transcendentals=blocks * rows * keys,
        ),
    )(*operands)


def joined(velocities, sums, shifts):
    top = functools.reduce(jnp.maximum, shifts)
    scales = [jnp.exp2(shift - top) for shift in shifts]
    summed = sum(s * scale for s, scale in zip(sums, scales))
    velocity = sum(v * scale for v, scale in zip(velocities, scales))
    return velocity, summed, top


def added(shares):
    stats = [share[CH:, :].astype(F32) for share in shares]
    return joined(
        [share[:CH, :].astype(F32) for share in shares],
        [s[0:1] + s[1:2] for s in stats],
        [s[2:3] + s[3:4] for s in stats],
    )


def add_kernel(here_ref, there_ref, out_ref):
    share = added([here_ref[1], there_ref[1]])
    out_ref[...] = message(*share, out_ref.shape[0], BF16)


def combine_kernel(gain_ref, here_ref, there_ref, beside_ref, out_ref):
    half = out_ref.shape[2]
    velocity, summed, _ = added([here_ref[0], there_ref[0], beside_ref[...]])
    velocity = (velocity * (gain_ref[0] / summed)).T
    velocity = velocity.reshape(out_ref.shape[0], 2, half, CH)
    velocity = jnp.concatenate([velocity[:, 0], velocity[:, 1]], axis=2).astype(BF16)
    for side in range(out_ref.shape[1]):
        out_ref[:, side] = velocity


def body(
    query_main, key_main, value_main, query_guide, key_guide, value_guide, map_main, map_guide
):
    tokens_here = query_main.shape[0]
    main_heads = query_main.shape[1] // HD
    guide_heads = query_guide.shape[1] // HD
    heads = main_heads + guide_heads
    head = lax.axis_index("zh")

    maps = jnp.concatenate([map_main, map_guide], axis=0).reshape(-1, HD, CH)
    map_t = lax.dynamic_index_in_dim(maps, head, 0, keepdims=False).T
    gain = jnp.where(head < main_heads, guidance, 1.0 - guidance).astype(F32).reshape(1)

    with jax.named_scope("pack"):
        packed = pl.pallas_call(
            functools.partial(pack_kernel, main_heads, guide_heads),
            in_specs=[VMEM] * 6,
            out_specs=VMEM,
            out_shape=jax.ShapeDtypeStruct((heads, 3, tokens_here, HD), BF16),
        )(query_main, key_main, value_main, query_guide, key_guide, value_guide)
    with jax.named_scope("to_heads"):
        arrived = exchange(packed, Z, PLANE_SETS)
    with jax.named_scope("gather"):
        q, kv = pl.pallas_call(
            copy_kernel,
            in_specs=[VMEM],
            out_specs=[VMEM] * 2,
            out_shape=[
                jax.ShapeDtypeStruct((heads * tokens_here, HD), BF16),
                jax.ShapeDtypeStruct((heads, 2, tokens_here, HD), BF16),
            ],
            compiler_params=SMALL,
        )(arrived)
        near = [kv] + [from_partner(kv, step, KEY_AXES) for step in NEAR_STEPS]
        far = [from_partner(kv, FAR_STEP, KEY_AXES)]
        beside = from_partner(q, Z0_STEP)
        across = [from_partner(q, Y_STEP), from_partner(q, Y_STEP ^ Z0_STEP)]
    with jax.named_scope("attend"):
        before = attend(across + [q, beside], near, map_t)
        there = from_partner(attend(across, far, map_t, before, 0), Y_STEP)
        here = attend([q, beside], far, map_t, before, len(across))
    with jax.named_scope("combine"):
        share = pl.pallas_call(
            add_kernel,
            in_specs=[VMEM] * 2,
            out_specs=VMEM,
            out_shape=jax.ShapeDtypeStruct(here.shape[1:], BF16),
            compiler_params=SMALL,
        )(here, there)
        velocity = pl.pallas_call(
            combine_kernel,
            in_specs=[SMEM] + [VMEM] * 3,
            out_specs=VMEM,
            out_shape=jax.ShapeDtypeStruct((heads, SIDES, tokens_here // 2, 2 * CH), BF16),
            compiler_params=SMALL,
        )(gain, here, there, from_partner(share, Z0_STEP))
    with jax.named_scope("to_tokens"):
        velocity = velocity.reshape((heads * SIDES,) + velocity.shape[2:])
        velocity = exchange(velocity, PLANE_AXES, SIDE_SETS)
        velocity = jnp.sum(velocity.astype(F32), axis=0)
        velocity = jnp.sum(lax.all_gather(velocity, "c", axis=0), axis=0)
    return velocity.reshape(tokens_here // 2, 2, CH).transpose(1, 0, 2).reshape(tokens_here, CH)


def solution(mesh):
    fine = Mesh(mesh.devices.reshape(4, 8, 2, 2, 2, 2), SEQ + GRP)
    placed = (P(SEQ, GRP),) * 6 + (P(GRP, None),) * 2
    return jax.shard_map(
        body, mesh=fine, in_specs=placed, out_specs=P(SEQ, None), check_vma=False
    )
```

```python
import functools
import math

import jax
import jax.numpy as jnp
from jax import lax
from jax.experimental import pallas as pl
from jax.experimental.pallas import tpu as pltpu
from jax.sharding import Mesh
from jax.sharding import PartitionSpec as P

HD = 128
CH = 64
guidance = 2.5
SCALE = math.log2(math.e) / math.sqrt(HD)
F32 = jnp.float32
BF16 = jnp.bfloat16
VMEM = pl.BlockSpec(memory_space=pltpu.VMEM)
SMEM = pl.BlockSpec(memory_space=pltpu.SMEM)
SMALL = pltpu.CompilerParams(vmem_limit_bytes=12 << 20)
MESSAGE_ROWS = CH + 16

SEQ = ("y", "zh", "z0", "xl")
GRP = ("xh", "c")
Z = ("zh", "z0")
PLANE_SETS = ([0, 2, 4, 6, 9, 11, 13, 15], [1, 3, 5, 7, 8, 10, 12, 14])
QUERY_AXES = ("y", "xl")
X_STEP, Y_STEP = 1, 2
KEY_AXES = ("y", "z0")
KEY_SETS = ([0, 1, 6, 7], [2, 3, 4, 5])
SIDES = 2
PLANE_AXES = Z + ("xh",)
SIDE_SETS = [[SIDES * z + x for z in planes for x in range(SIDES)] for planes in PLANE_SETS]


def exchange(x, axes, sets):
    return lax.all_to_all(x, axes, 0, 0, tiled=True, axis_index_groups=sets)


def from_partner(x, step):
    size = lax.axis_size(QUERY_AXES)
    return lax.ppermute(x, QUERY_AXES, [(i, i ^ step) for i in range(size)])


def dot_t(a, b):
    return lax.dot_general(a, b, (((1,), (1,)), ((), ())), preferred_element_type=F32)


def pack_kernel(main_heads, guide_heads, qm, km, vm, qg, kg, vg, out_ref):
    for h in range(main_heads + guide_heads):
        at = (h if h < main_heads else h - main_heads) * HD
        for t, ref in enumerate((qm, km, vm) if h < main_heads else (qg, kg, vg)):
            out_ref[h, t] = ref[:, at : at + HD]


def copy_kernel(in_ref, q_ref, copies_ref):
    heads, _, tokens, _ = in_ref.shape
    for h in range(heads):
        q_ref[h * tokens : (h + 1) * tokens, :] = in_ref[h, 0]
        for copy in range(copies_ref.shape[0]):
            copies_ref[copy, h] = in_ref[h, 1:]


def split_two(x):
    high = x.astype(BF16).astype(F32)
    return high, x - high


def attend_kernel(*refs):
    *q_refs, kv_ref, map_ref, out_ref, staged_ref, sums_ref = refs
    rows = out_ref.shape[2]
    for k, q_ref in enumerate(q_refs):
        staged_ref[k] = q_ref[...]

    def all_pieces(which):
        return kv_ref[:, which].reshape(-1, HD)

    def weighted(queries, shift):
        scores = dot_t(queries, all_pieces(0)) * SCALE
        if shift is not None:
            scores = scores - shift
        values = all_pieces(1)
        values = jnp.concatenate([values, jnp.ones_like(values)], axis=1)
        weights = jnp.exp2(scores).astype(BF16)
        return jnp.dot(weights, values, preferred_element_type=F32)

    def emit(k, at, total, shift):
        count = total.shape[0]
        lane = lax.broadcasted_iota(jnp.int32, (count, HD), 1)
        picks = lax.broadcasted_iota(jnp.int32, (16, HD), 0) == lax.broadcasted_iota(
            jnp.int32, (16, HD), 1
        )
        out_ref[k, :CH, at] = dot_t(map_ref[...], total[:, :HD].astype(BF16)).astype(BF16)
        high, low = split_two(total[:, HD:])
        rest = jnp.where(lane == 0, high, jnp.where(lane == 1, low, 0.0))
        if shift is not None:
            high, low = split_two(shift)
            rest = jnp.where(lane == 2, high, jnp.where(lane == 3, low, rest))
        rest = dot_t(picks.astype(F32).astype(BF16), rest.astype(BF16))
        out_ref[k, CH:, at] = rest.astype(BF16)

    @pl.loop(0, len(q_refs))
    def _(k):
        total = weighted(staged_ref[k], None)
        emit(k, slice(None), total, None)
        sums_ref[...] = total[:, HD:]
        least = jnp.min(sums_ref[...])
        most = jnp.max(sums_ref[...])

        @pl.when(jnp.logical_not((least > 1e-20) & (most < 1e25)))
        def _():
            @pl.loop(0, rows // HD)
            def _(i):
                at = pl.ds(pl.multiple_of(i * HD, HD), HD)
                queries = staged_ref[k, at, :]
                top = jnp.max(dot_t(queries, all_pieces(0)), axis=1, keepdims=True)
                shift = jnp.ceil(top * SCALE)
                emit(k, at, weighted(queries, shift), shift)


def attend(queries, key_values, map_t):
    rows = queries[0].shape[0]
    keys = key_values.shape[0] * key_values.shape[2]
    blocks = len(queries)
    return pl.pallas_call(
        attend_kernel,
        in_specs=[VMEM] * (2 + blocks),
        out_specs=VMEM,
        out_shape=jax.ShapeDtypeStruct((blocks, MESSAGE_ROWS, rows), BF16),
        scratch_shapes=[pltpu.VMEM((blocks, rows, HD), BF16), pltpu.VMEM((rows, HD), F32)],
        compiler_params=pltpu.CompilerParams(vmem_limit_bytes=40 << 20),
        cost_estimate=pl.CostEstimate(
            flops=8 * blocks * rows * keys * HD,
            bytes_accessed=2 << 20,
            transcendentals=blocks * rows * keys,
        ),
    )(*queries, key_values, map_t)


def added(shares):
    stats = [share[CH:, :].astype(F32) for share in shares]
    shifts = [s[2:3] + s[3:4] for s in stats]
    top = functools.reduce(jnp.maximum, shifts)
    scales = [jnp.exp2(shift - top) for shift in shifts]
    summed = sum((s[0:1] + s[1:2]) * scale for s, scale in zip(stats, scales))
    velocity = sum(share[:CH, :].astype(F32) * scale for share, scale in zip(shares, scales))
    return velocity, summed, top


def add_kernel(here_ref, there_ref, out_ref):
    velocity, summed, top = added([here_ref[1], there_ref[1]])
    out_ref[:CH, :] = velocity.astype(BF16)
    tail = split_two(summed) + split_two(top)
    filler = jnp.zeros((out_ref.shape[0] - CH - len(tail), out_ref.shape[1]), F32)
    out_ref[CH:, :] = jnp.concatenate(tail + (filler,), axis=0).astype(BF16)


def combine_kernel(gain_ref, here_ref, there_ref, beside_ref, out_ref):
    half = out_ref.shape[2]
    velocity, summed, _ = added([here_ref[0], there_ref[0], beside_ref[...]])
    velocity = (velocity * (gain_ref[0] / summed)).T
    velocity = velocity.reshape(out_ref.shape[0], 2, half, CH)
    velocity = jnp.concatenate([velocity[:, 0], velocity[:, 1]], axis=2).astype(BF16)
    for side in range(out_ref.shape[1]):
        out_ref[:, side] = velocity


def body(
    query_main, key_main, value_main, query_guide, key_guide, value_guide, map_main, map_guide
):
    tokens_here = query_main.shape[0]
    main_heads = query_main.shape[1] // HD
    guide_heads = query_guide.shape[1] // HD
    heads = main_heads + guide_heads
    head = lax.axis_index("zh")

    maps = jnp.concatenate([map_main, map_guide], axis=0).reshape(-1, HD, CH)
    map_t = lax.dynamic_index_in_dim(maps, head, 0, keepdims=False).T
    gain = jnp.where(head < main_heads, guidance, 1.0 - guidance).astype(F32).reshape(1)

    with jax.named_scope("pack"):
        packed = pl.pallas_call(
            functools.partial(pack_kernel, main_heads, guide_heads),
            in_specs=[VMEM] * 6,
            out_specs=VMEM,
            out_shape=jax.ShapeDtypeStruct((heads, 3, tokens_here, HD), BF16),
        )(query_main, key_main, value_main, query_guide, key_guide, value_guide)
    with jax.named_scope("to_heads"):
        arrived = exchange(packed, Z, PLANE_SETS)
    with jax.named_scope("gather"):
        copies = (len(KEY_SETS[0]), heads, 2, tokens_here, HD)
        q, copies = pl.pallas_call(
            copy_kernel,
            in_specs=[VMEM],
            out_specs=[VMEM] * 2,
            out_shape=[
                jax.ShapeDtypeStruct((heads * tokens_here, HD), BF16),
                jax.ShapeDtypeStruct(copies, BF16),
            ],
            compiler_params=SMALL,
        )(arrived)
        key_values = exchange(copies.reshape((-1,) + copies.shape[2:]), KEY_AXES, KEY_SETS)
        beside = from_partner(q, X_STEP)
        across = [from_partner(q, Y_STEP), from_partner(q, Y_STEP ^ X_STEP)]
    with jax.named_scope("attend"):
        there = from_partner(attend(across, key_values, map_t), Y_STEP)
        here = attend([q, beside], key_values, map_t)
    with jax.named_scope("combine"):
        share = pl.pallas_call(
            add_kernel,
            in_specs=[VMEM] * 2,
            out_specs=VMEM,
            out_shape=jax.ShapeDtypeStruct(here.shape[1:], BF16),
            compiler_params=SMALL,
        )(here, there)
        velocity = pl.pallas_call(
            combine_kernel,
            in_specs=[SMEM] + [VMEM] * 3,
            out_specs=VMEM,
            out_shape=jax.ShapeDtypeStruct((heads, SIDES, tokens_here // 2, 2 * CH), BF16),
            compiler_params=SMALL,
        )(gain, here, there, from_partner(share, X_STEP))
    with jax.named_scope("to_tokens"):
        velocity = velocity.reshape((heads * SIDES,) + velocity.shape[2:])
        velocity = exchange(velocity, PLANE_AXES, SIDE_SETS)
        velocity = jnp.sum(velocity.astype(F32), axis=0)
        velocity = jnp.sum(lax.all_gather(velocity, "c", axis=0), axis=0)
    return velocity.reshape(tokens_here // 2, 2, CH).transpose(1, 0, 2).reshape(tokens_here, CH)


def solution(mesh):
    fine = Mesh(mesh.devices.reshape(4, 8, 2, 2, 2, 2), SEQ + GRP)
    placed = (P(SEQ, GRP),) * 6 + (P(GRP, None),) * 2
    return jax.shard_map(
        body, mesh=fine, in_specs=placed, out_specs=P(SEQ, None), check_vma=False
    )
```

```python
import functools
import math

import jax
import jax.numpy as jnp
from jax import lax
from jax.experimental import pallas as pl
from jax.experimental.pallas import tpu as pltpu
from jax.sharding import Mesh
from jax.sharding import PartitionSpec as P

HD = 128
CH = 64
guidance = 2.5
SCALE = math.log2(math.e) / math.sqrt(HD)
F32 = jnp.float32
BF16 = jnp.bfloat16
VMEM = pl.BlockSpec(memory_space=pltpu.VMEM)
SMEM = pl.BlockSpec(memory_space=pltpu.SMEM)
SMALL = pltpu.CompilerParams(vmem_limit_bytes=12 << 20)
MESSAGE_ROWS = CH + 16

SEQ = ("y", "zh", "z0", "xl")
GRP = ("xh", "c")
Z = ("zh", "z0")
PLANE_SETS = ([0, 2, 4, 6, 9, 11, 13, 15], [1, 3, 5, 7, 8, 10, 12, 14])
QUERY_AXES = ("y", "z0")
Z0_STEP, Y_STEP = 1, 6
KEY_AXES = ("y", "xl")
KEY_SETS = ([0, 1, 2, 3], [4, 5, 6, 7])
SIDES = 2
PLANE_AXES = Z + ("xh",)
SIDE_SETS = [[SIDES * z + x for z in planes for x in range(SIDES)] for planes in PLANE_SETS]


def exchange(x, axes, sets):
    return lax.all_to_all(x, axes, 0, 0, tiled=True, axis_index_groups=sets)


def from_partner(x, step):
    size = lax.axis_size(QUERY_AXES)
    return lax.ppermute(x, QUERY_AXES, [(i, i ^ step) for i in range(size)])


def dot_t(a, b):
    return lax.dot_general(a, b, (((1,), (1,)), ((), ())), preferred_element_type=F32)


def pack_kernel(main_heads, guide_heads, qm, km, vm, qg, kg, vg, out_ref):
    for h in range(main_heads + guide_heads):
        at = (h if h < main_heads else h - main_heads) * HD
        for t, ref in enumerate((qm, km, vm) if h < main_heads else (qg, kg, vg)):
            out_ref[h, t] = ref[:, at : at + HD]


def copy_kernel(in_ref, q_ref, copies_ref):
    heads, _, tokens, _ = in_ref.shape
    for h in range(heads):
        q_ref[h * tokens : (h + 1) * tokens, :] = in_ref[h, 0]
        for copy in range(copies_ref.shape[0]):
            copies_ref[copy, h] = in_ref[h, 1:]


def split_two(x):
    high = x.astype(BF16).astype(F32)
    return high, x - high


def message(velocity, summed, top, rows, dtype):
    tail = split_two(summed) + split_two(top) if dtype == BF16 else (summed, top)
    filler = jnp.zeros((rows - CH - len(tail), velocity.shape[1]), F32)
    return jnp.concatenate((velocity,) + tail + (filler,), axis=0).astype(dtype)


def attend_kernel(count, first_before, *refs):
    q_refs, refs = refs[:count], refs[count:]
    if first_before is None:
        arrived_ref, map_ref, out_ref, staged_ref, sums_ref = refs
        before_ref = None
    else:
        own_ref, kv_ref, map_ref, before_ref, out_ref, staged_ref, sums_ref = refs
    rows = out_ref.shape[2]
    for k, q_ref in enumerate(q_refs):
        staged_ref[k] = q_ref[...]

    def all_pieces(which):
        if first_before is None:
            return arrived_ref[:, 1 + which].reshape(-1, HD)
        blocks = len(KEY_SETS[0])
        size = kv_ref.shape[0] // blocks
        starts = [(own_ref[0] ^ i) * size for i in range(1, blocks)]
        pieces = [kv_ref[pl.ds(start, size), which].reshape(-1, HD) for start in starts]
        return jnp.concatenate(pieces, axis=0)

    def weighted(queries, shift):
        scores = dot_t(queries, all_pieces(0)) * SCALE
        if shift is not None:
            scores = scores - shift
        values = all_pieces(1)
        values = jnp.concatenate([values, jnp.ones_like(values)], axis=1)
        weights = jnp.exp2(scores).astype(BF16)
        return jnp.dot(weights, values, preferred_element_type=F32)

    def emit(k, at, total, shift):
        count = total.shape[0]
        lane = lax.broadcasted_iota(jnp.int32, (count, HD), 1)
        picks = lax.broadcasted_iota(jnp.int32, (16, HD), 0) == lax.broadcasted_iota(
            jnp.int32, (16, HD), 1
        )
        velocity = dot_t(map_ref[...], total[:, :HD].astype(BF16))
        high, low = split_two(total[:, HD:])
        rest = jnp.where(lane == 0, high, jnp.where(lane == 1, low, 0.0))
        if shift is not None:
            high, low = split_two(shift)
            rest = jnp.where(lane == 2, high, jnp.where(lane == 3, low, rest))
        rest = dot_t(picks.astype(F32).astype(BF16), rest.astype(BF16))
        summed, top = rest[0:1] + rest[1:2], rest[2:3] + rest[3:4]
        if before_ref is not None:
            before = before_ref[first_before + k, :, at]
            velocity, summed, top = joined(
                [velocity, before[:CH]], [summed, before[CH : CH + 1]], [top, before[CH + 1 : CH + 2]]
            )
        out_ref[k, :, at] = message(velocity, summed, top, out_ref.shape[1], out_ref.dtype)

    @pl.loop(0, len(q_refs))
    def _(k):
        total = weighted(staged_ref[k], None)
        emit(k, slice(None), total, None)
        sums_ref[...] = total[:, HD:]
        least = jnp.min(sums_ref[...])
        most = jnp.max(sums_ref[...])

        @pl.when(jnp.logical_not((least > 1e-20) & (most < 1e25)))
        def _():
            @pl.loop(0, rows // HD)
            def _(i):
                at = pl.ds(pl.multiple_of(i * HD, HD), HD)
                queries = staged_ref[k, at, :]
                top = jnp.max(dot_t(queries, all_pieces(0)), axis=1, keepdims=True)
                shift = jnp.ceil(top * SCALE)
                emit(k, at, weighted(queries, shift), shift)


def attend(queries, keys_in, map_t, first_before=None):
    rows = queries[0].shape[0]
    blocks = len(queries)
    last = first_before is not None
    keys = rows * (len(KEY_SETS[0]) - 1 if last else 1)
    operands = [*queries, *keys_in[:2], map_t, *keys_in[2:]]
    specs = [VMEM] * len(operands)
    if last:
        specs[blocks] = SMEM
    out = (blocks, MESSAGE_ROWS, rows) if last else (blocks, CH + 8, rows)
    return pl.pallas_call(
        functools.partial(attend_kernel, blocks, first_before),
        in_specs=specs,
        out_specs=VMEM,
        out_shape=jax.ShapeDtypeStruct(out, BF16 if last else F32),
        scratch_shapes=[pltpu.VMEM((blocks, rows, HD), BF16), pltpu.VMEM((rows, HD), F32)],
        compiler_params=pltpu.CompilerParams(vmem_limit_bytes=40 << 20),
        cost_estimate=pl.CostEstimate(
            flops=8 * blocks * rows * keys * HD,
            bytes_accessed=2 << 20,
            transcendentals=blocks * rows * keys,
        ),
    )(*operands)


def joined(velocities, sums, shifts):
    top = functools.reduce(jnp.maximum, shifts)
    scales = [jnp.exp2(shift - top) for shift in shifts]
    summed = sum(s * scale for s, scale in zip(sums, scales))
    velocity = sum(v * scale for v, scale in zip(velocities, scales))
    return velocity, summed, top


def added(shares):
    stats = [share[CH:, :].astype(F32) for share in shares]
    return joined(
        [share[:CH, :].astype(F32) for share in shares],
        [s[0:1] + s[1:2] for s in stats],
        [s[2:3] + s[3:4] for s in stats],
    )


def add_kernel(here_ref, there_ref, out_ref):
    share = added([here_ref[1], there_ref[1]])
    out_ref[...] = message(*share, out_ref.shape[0], BF16)


def combine_kernel(gain_ref, here_ref, there_ref, beside_ref, out_ref):
    half = out_ref.shape[2]
    velocity, summed, _ = added([here_ref[0], there_ref[0], beside_ref[...]])
    velocity = (velocity * (gain_ref[0] / summed)).T
    velocity = velocity.reshape(out_ref.shape[0], 2, half, CH)
    velocity = jnp.concatenate([velocity[:, 0], velocity[:, 1]], axis=2).astype(BF16)
    for side in range(out_ref.shape[1]):
        out_ref[:, side] = velocity


def body(
    query_main, key_main, value_main, query_guide, key_guide, value_guide, map_main, map_guide
):
    tokens_here = query_main.shape[0]
    main_heads = query_main.shape[1] // HD
    guide_heads = query_guide.shape[1] // HD
    heads = main_heads + guide_heads
    head = lax.axis_index("zh")

    maps = jnp.concatenate([map_main, map_guide], axis=0).reshape(-1, HD, CH)
    map_t = lax.dynamic_index_in_dim(maps, head, 0, keepdims=False).T
    gain = jnp.where(head < main_heads, guidance, 1.0 - guidance).astype(F32).reshape(1)

    with jax.named_scope("pack"):
        packed = pl.pallas_call(
            functools.partial(pack_kernel, main_heads, guide_heads),
            in_specs=[VMEM] * 6,
            out_specs=VMEM,
            out_shape=jax.ShapeDtypeStruct((heads, 3, tokens_here, HD), BF16),
        )(query_main, key_main, value_main, query_guide, key_guide, value_guide)
    with jax.named_scope("to_heads"):
        arrived = exchange(packed, Z, PLANE_SETS)
    with jax.named_scope("gather"):
        copies = (len(KEY_SETS[0]), heads, 2, tokens_here, HD)
        q, copies = pl.pallas_call(
            copy_kernel,
            in_specs=[VMEM],
            out_specs=[VMEM] * 2,
            out_shape=[
                jax.ShapeDtypeStruct((heads * tokens_here, HD), BF16),
                jax.ShapeDtypeStruct(copies, BF16),
            ],
            compiler_params=SMALL,
        )(arrived)
        key_values = exchange(copies.reshape((-1,) + copies.shape[2:]), KEY_AXES, KEY_SETS)
        beside = from_partner(q, Z0_STEP)
        across = [from_partner(q, Y_STEP), from_partner(q, Y_STEP ^ Z0_STEP)]
    with jax.named_scope("attend"):
        before = attend(across + [q, beside], [arrived], map_t)
        own = lax.axis_index(KEY_AXES).astype(jnp.int32) & 3
        others = [own.reshape(1), key_values, before]
        there = from_partner(attend(across, others, map_t, 0), Y_STEP)
        here = attend([q, beside], others, map_t, len(across))
    with jax.named_scope("combine"):
        share = pl.pallas_call(
            add_kernel,
            in_specs=[VMEM] * 2,
            out_specs=VMEM,
            out_shape=jax.ShapeDtypeStruct(here.shape[1:], BF16),
            compiler_params=SMALL,
        )(here, there)
        velocity = pl.pallas_call(
            combine_kernel,
            in_specs=[SMEM] + [VMEM] * 3,
            out_specs=VMEM,
            out_shape=jax.ShapeDtypeStruct((heads, SIDES, tokens_here // 2, 2 * CH), BF16),
            compiler_params=SMALL,
        )(gain, here, there, from_partner(share, Z0_STEP))
    with jax.named_scope("to_tokens"):
        velocity = velocity.reshape((heads * SIDES,) + velocity.shape[2:])
        velocity = exchange(velocity, PLANE_AXES, SIDE_SETS)
        velocity = jnp.sum(velocity.astype(F32), axis=0)
        velocity = jnp.sum(lax.all_gather(velocity, "c", axis=0), axis=0)
    return velocity.reshape(tokens_here // 2, 2, CH).transpose(1, 0, 2).reshape(tokens_here, CH)


def solution(mesh):
    fine = Mesh(mesh.devices.reshape(4, 8, 2, 2, 2, 2), SEQ + GRP)
    placed = (P(SEQ, GRP),) * 6 + (P(GRP, None),) * 2
    return jax.shard_map(
        body, mesh=fine, in_specs=placed, out_specs=P(SEQ, None), check_vma=False
    )
```

```python
import functools
import math

import jax
import jax.numpy as jnp
from jax import lax
from jax.experimental import pallas as pl
from jax.experimental.pallas import tpu as pltpu
from jax.sharding import Mesh
from jax.sharding import PartitionSpec as P

HD = 128
CH = 64
guidance = 2.5
SCALE = math.log2(math.e) / math.sqrt(HD)
F32 = jnp.float32
BF16 = jnp.bfloat16
VMEM = pl.BlockSpec(memory_space=pltpu.VMEM)
SMEM = pl.BlockSpec(memory_space=pltpu.SMEM)
SMALL = pltpu.CompilerParams(vmem_limit_bytes=12 << 20)
MESSAGE_ROWS = CH + 16

SEQ = ("y", "zh", "z0", "xl")
GRP = ("xh", "c")
Z = ("zh", "z0")
PLANE_SETS = ([0, 2, 4, 6, 9, 11, 13, 15], [1, 3, 5, 7, 8, 10, 12, 14])
QUERY_AXES = ("y", "z0")
Z0_STEP, Y_STEP = 1, 6
KEY_AXES = ("y", "xl")
KEY_STEPS = (1, 2, 3)
SIDES = 2
PLANE_AXES = Z + ("xh",)
SIDE_SETS = [[SIDES * z + x for z in planes for x in range(SIDES)] for planes in PLANE_SETS]


def exchange(x, axes, sets):
    return lax.all_to_all(x, axes, 0, 0, tiled=True, axis_index_groups=sets)


def from_partner(x, step, axes=QUERY_AXES):
    return lax.ppermute(x, axes, [(i, i ^ step) for i in range(lax.axis_size(axes))])


def dot_t(a, b):
    return lax.dot_general(a, b, (((1,), (1,)), ((), ())), preferred_element_type=F32)


def pack_kernel(main_heads, guide_heads, qm, km, vm, qg, kg, vg, out_ref):
    for h in range(main_heads + guide_heads):
        at = (h if h < main_heads else h - main_heads) * HD
        for t, ref in enumerate((qm, km, vm) if h < main_heads else (qg, kg, vg)):
            out_ref[h, t] = ref[:, at : at + HD]


def copy_kernel(in_ref, q_ref, kv_ref):
    heads, _, tokens, _ = in_ref.shape
    for h in range(heads):
        q_ref[h * tokens : (h + 1) * tokens, :] = in_ref[h, 0]
        kv_ref[h] = in_ref[h, 1:]


def split_two(x):
    high = x.astype(BF16).astype(F32)
    return high, x - high


def attend_kernel(count, *refs):
    q_refs, refs = refs[:count], refs[count:]
    *kv_refs, map_ref, out_ref, staged_ref, sums_ref = refs
    rows = out_ref.shape[2]
    for k, q_ref in enumerate(q_refs):
        staged_ref[k] = q_ref[...]

    def all_pieces(which):
        return jnp.concatenate([ref[:, which].reshape(-1, HD) for ref in kv_refs], axis=0)

    def weighted(queries, shift):
        scores = dot_t(queries, all_pieces(0)) * SCALE
        if shift is not None:
            scores = scores - shift
        values = all_pieces(1)
        values = jnp.concatenate([values, jnp.ones_like(values)], axis=1)
        weights = jnp.exp2(scores).astype(BF16)
        return jnp.dot(weights, values, preferred_element_type=F32)

    def emit(k, at, total, shift):
        count = total.shape[0]
        lane = lax.broadcasted_iota(jnp.int32, (count, HD), 1)
        picks = lax.broadcasted_iota(jnp.int32, (16, HD), 0) == lax.broadcasted_iota(
            jnp.int32, (16, HD), 1
        )
        out_ref[k, :CH, at] = dot_t(map_ref[...], total[:, :HD].astype(BF16)).astype(BF16)
        high, low = split_two(total[:, HD:])
        rest = jnp.where(lane == 0, high, jnp.where(lane == 1, low, 0.0))
        if shift is not None:
            high, low = split_two(shift)
            rest = jnp.where(lane == 2, high, jnp.where(lane == 3, low, rest))
        rest = dot_t(picks.astype(F32).astype(BF16), rest.astype(BF16))
        out_ref[k, CH:, at] = rest.astype(BF16)

    @pl.loop(0, len(q_refs))
    def _(k):
        total = weighted(staged_ref[k], None)
        emit(k, slice(None), total, None)
        sums_ref[...] = total[:, HD:]
        least = jnp.min(sums_ref[...])
        most = jnp.max(sums_ref[...])

        @pl.when(jnp.logical_not((least > 1e-20) & (most < 1e25)))
        def _():
            @pl.loop(0, rows // HD)
            def _(i):
                at = pl.ds(pl.multiple_of(i * HD, HD), HD)
                queries = staged_ref[k, at, :]
                top = jnp.max(dot_t(queries, all_pieces(0)), axis=1, keepdims=True)
                shift = jnp.ceil(top * SCALE)
                emit(k, at, weighted(queries, shift), shift)


def attend(queries, key_values, map_t):
    rows = queries[0].shape[0]
    keys = key_values[0].shape[0] * key_values[0].shape[2] * len(key_values)
    blocks = len(queries)
    return pl.pallas_call(
        functools.partial(attend_kernel, blocks),
        in_specs=[VMEM] * (1 + blocks + len(key_values)),
        out_specs=VMEM,
        out_shape=jax.ShapeDtypeStruct((blocks, MESSAGE_ROWS, rows), BF16),
        scratch_shapes=[pltpu.VMEM((blocks, rows, HD), BF16), pltpu.VMEM((rows, HD), F32)],
        compiler_params=pltpu.CompilerParams(vmem_limit_bytes=40 << 20),
        cost_estimate=pl.CostEstimate(
            flops=8 * blocks * rows * keys * HD,
            bytes_accessed=2 << 20,
            transcendentals=blocks * rows * keys,
        ),
    )(*queries, *key_values, map_t)


def added(shares):
    stats = [share[CH:, :].astype(F32) for share in shares]
    shifts = [s[2:3] + s[3:4] for s in stats]
    top = functools.reduce(jnp.maximum, shifts)
    scales = [jnp.exp2(shift - top) for shift in shifts]
    summed = sum((s[0:1] + s[1:2]) * scale for s, scale in zip(stats, scales))
    velocity = sum(share[:CH, :].astype(F32) * scale for share, scale in zip(shares, scales))
    return velocity, summed, top


def add_kernel(here_ref, there_ref, out_ref):
    velocity, summed, top = added([here_ref[1], there_ref[1]])
    out_ref[:CH, :] = velocity.astype(BF16)
    tail = split_two(summed) + split_two(top)
    filler = jnp.zeros((out_ref.shape[0] - CH - len(tail), out_ref.shape[1]), F32)
    out_ref[CH:, :] = jnp.concatenate(tail + (filler,), axis=0).astype(BF16)


def combine_kernel(gain_ref, here_ref, there_ref, beside_ref, out_ref):
    half = out_ref.shape[2]
    velocity, summed, _ = added([here_ref[0], there_ref[0], beside_ref[...]])
    velocity = (velocity * (gain_ref[0] / summed)).T
    velocity = velocity.reshape(out_ref.shape[0], 2, half, CH)
    velocity = jnp.concatenate([velocity[:, 0], velocity[:, 1]], axis=2).astype(BF16)
    for side in range(out_ref.shape[1]):
        out_ref[:, side] = velocity


def body(
    query_main, key_main, value_main, query_guide, key_guide, value_guide, map_main, map_guide
):
    tokens_here = query_main.shape[0]
    main_heads = query_main.shape[1] // HD
    guide_heads = query_guide.shape[1] // HD
    heads = main_heads + guide_heads
    head = lax.axis_index("zh")

    maps = jnp.concatenate([map_main, map_guide], axis=0).reshape(-1, HD, CH)
    map_t = lax.dynamic_index_in_dim(maps, head, 0, keepdims=False).T
    gain = jnp.where(head < main_heads, guidance, 1.0 - guidance).astype(F32).reshape(1)

    with jax.named_scope("pack"):
        packed = pl.pallas_call(
            functools.partial(pack_kernel, main_heads, guide_heads),
            in_specs=[VMEM] * 6,
            out_specs=VMEM,
            out_shape=jax.ShapeDtypeStruct((heads, 3, tokens_here, HD), BF16),
        )(query_main, key_main, value_main, query_guide, key_guide, value_guide)
    with jax.named_scope("to_heads"):
        arrived = exchange(packed, Z, PLANE_SETS)
    with jax.named_scope("gather"):
        q, kv = pl.pallas_call(
            copy_kernel,
            in_specs=[VMEM],
            out_specs=[VMEM] * 2,
            out_shape=[
                jax.ShapeDtypeStruct((heads * tokens_here, HD), BF16),
                jax.ShapeDtypeStruct((heads, 2, tokens_here, HD), BF16),
            ],
            compiler_params=SMALL,
        )(arrived)
        key_values = [kv] + [from_partner(kv, step, KEY_AXES) for step in KEY_STEPS]
        beside = from_partner(q, Z0_STEP)
        across = [from_partner(q, Y_STEP), from_partner(q, Y_STEP ^ Z0_STEP)]
    with jax.named_scope("attend"):
        there = from_partner(attend(across, key_values, map_t), Y_STEP)
        here = attend([q, beside], key_values, map_t)
    with jax.named_scope("combine"):
        share = pl.pallas_call(
            add_kernel,
            in_specs=[VMEM] * 2,
            out_specs=VMEM,
            out_shape=jax.ShapeDtypeStruct(here.shape[1:], BF16),
            compiler_params=SMALL,
        )(here, there)
        velocity = pl.pallas_call(
            combine_kernel,
            in_specs=[SMEM] + [VMEM] * 3,
            out_specs=VMEM,
            out_shape=jax.ShapeDtypeStruct((heads, SIDES, tokens_here // 2, 2 * CH), BF16),
            compiler_params=SMALL,
        )(gain, here, there, from_partner(share, Z0_STEP))
    with jax.named_scope("to_tokens"):
        velocity = velocity.reshape((heads * SIDES,) + velocity.shape[2:])
        velocity = exchange(velocity, PLANE_AXES, SIDE_SETS)
        velocity = jnp.sum(velocity.astype(F32), axis=0)
        velocity = jnp.sum(lax.all_gather(velocity, "c", axis=0), axis=0)
    return velocity.reshape(tokens_here // 2, 2, CH).transpose(1, 0, 2).reshape(tokens_here, CH)


def solution(mesh):
    fine = Mesh(mesh.devices.reshape(4, 8, 2, 2, 2, 2), SEQ + GRP)
    placed = (P(SEQ, GRP),) * 6 + (P(GRP, None),) * 2
    return jax.shard_map(
        body, mesh=fine, in_specs=placed, out_specs=P(SEQ, None), check_vma=False
    )
```

```python
import functools
import math

import jax
import jax.numpy as jnp
from jax import lax
from jax.experimental import pallas as pl
from jax.experimental.pallas import tpu as pltpu
from jax.sharding import Mesh
from jax.sharding import PartitionSpec as P

HD = 128
CH = 64
guidance = 2.5
SCALE = math.log2(math.e) / math.sqrt(HD)
F32 = jnp.float32
BF16 = jnp.bfloat16
VMEM = pl.BlockSpec(memory_space=pltpu.VMEM)
SMEM = pl.BlockSpec(memory_space=pltpu.SMEM)
SMALL = pltpu.CompilerParams(vmem_limit_bytes=12 << 20)
MESSAGE_ROWS = CH + 16

SEQ = ("y", "zh", "z0", "xl")
GRP = ("xh", "c")
Z = ("zh", "z0")
PLANE_SETS = ([0, 2, 4, 6, 9, 11, 13, 15], [1, 3, 5, 7, 8, 10, 12, 14])
QUERY_AXES = ("y", "z0")
Z0_STEP, Y_STEP = 1, 6
KEY_AXES = ("y", "xl")
KEY_SETS = ([0, 1, 2, 3], [4, 5, 6, 7])
SIDES = 2
PLANE_AXES = Z + ("xh",)
SIDE_SETS = [[SIDES * z + x for z in planes for x in range(SIDES)] for planes in PLANE_SETS]


def exchange(x, axes, sets):
    return lax.all_to_all(x, axes, 0, 0, tiled=True, axis_index_groups=sets)


def from_partner(x, step):
    size = lax.axis_size(QUERY_AXES)
    return lax.ppermute(x, QUERY_AXES, [(i, i ^ step) for i in range(size)])


def dot_t(a, b):
    return lax.dot_general(a, b, (((1,), (1,)), ((), ())), preferred_element_type=F32)


def pack_kernel(main_heads, guide_heads, qm, km, vm, qg, kg, vg, out_ref):
    for h in range(main_heads + guide_heads):
        at = (h if h < main_heads else h - main_heads) * HD
        for t, ref in enumerate((qm, km, vm) if h < main_heads else (qg, kg, vg)):
            out_ref[h, t] = ref[:, at : at + HD]


def copy_kernel(in_ref, q_ref, copies_ref):
    heads, _, tokens, _ = in_ref.shape
    for h in range(heads):
        q_ref[h * tokens : (h + 1) * tokens, :] = in_ref[h, 0]
        for copy in range(copies_ref.shape[0]):
            copies_ref[copy, h] = in_ref[h, 1:]


def split_two(x):
    high = x.astype(BF16).astype(F32)
    return high, x - high


def attend_kernel(*refs):
    *q_refs, kv_ref, map_ref, out_ref, staged_ref, sums_ref = refs
    rows = out_ref.shape[2]
    for k, q_ref in enumerate(q_refs):
        staged_ref[k] = q_ref[...]

    def all_pieces(which):
        return kv_ref[:, which].reshape(-1, HD)

    def weighted(queries, shift):
        scores = dot_t(queries, all_pieces(0)) * SCALE
        if shift is not None:
            scores = scores - shift
        values = all_pieces(1)
        values = jnp.concatenate([values, jnp.ones_like(values)], axis=1)
        weights = jnp.exp2(scores).astype(BF16)
        return jnp.dot(weights, values, preferred_element_type=F32)

    def emit(k, at, total, shift):
        count = total.shape[0]
        lane = lax.broadcasted_iota(jnp.int32, (count, HD), 1)
        picks = lax.broadcasted_iota(jnp.int32, (16, HD), 0) == lax.broadcasted_iota(
            jnp.int32, (16, HD), 1
        )
        out_ref[k, :CH, at] = dot_t(map_ref[...], total[:, :HD].astype(BF16)).astype(BF16)
        high, low = split_two(total[:, HD:])
        rest = jnp.where(lane == 0, high, jnp.where(lane == 1, low, 0.0))
        if shift is not None:
            high, low = split_two(shift)
            rest = jnp.where(lane == 2, high, jnp.where(lane == 3, low, rest))
        rest = dot_t(picks.astype(F32).astype(BF16), rest.astype(BF16))
        out_ref[k, CH:, at] = rest.astype(BF16)

    @pl.loop(0, len(q_refs))
    def _(k):
        total = weighted(staged_ref[k], None)
        emit(k, slice(None), total, None)
        sums_ref[...] = total[:, HD:]
        least = jnp.min(sums_ref[...])
        most = jnp.max(sums_ref[...])

        @pl.when(jnp.logical_not((least > 1e-20) & (most < 1e25)))
        def _():
            @pl.loop(0, rows // HD)
            def _(i):
                at = pl.ds(pl.multiple_of(i * HD, HD), HD)
                queries = staged_ref[k, at, :]
                top = jnp.max(dot_t(queries, all_pieces(0)), axis=1, keepdims=True)
                shift = jnp.ceil(top * SCALE)
                emit(k, at, weighted(queries, shift), shift)


def attend(queries, key_values, map_t):
    rows = queries[0].shape[0]
    keys = key_values.shape[0] * key_values.shape[2]
    blocks = len(queries)
    return pl.pallas_call(
        attend_kernel,
        in_specs=[VMEM] * (2 + blocks),
        out_specs=VMEM,
        out_shape=jax.ShapeDtypeStruct((blocks, MESSAGE_ROWS, rows), BF16),
        scratch_shapes=[pltpu.VMEM((blocks, rows, HD), BF16), pltpu.VMEM((rows, HD), F32)],
        compiler_params=pltpu.CompilerParams(vmem_limit_bytes=40 << 20),
        cost_estimate=pl.CostEstimate(
            flops=8 * blocks * rows * keys * HD,
            bytes_accessed=2 << 20,
            transcendentals=blocks * rows * keys,
        ),
    )(*queries, key_values, map_t)


def added(shares):
    stats = [share[CH:, :].astype(F32) for share in shares]
    shifts = [s[2:3] + s[3:4] for s in stats]
    top = functools.reduce(jnp.maximum, shifts)
    scales = [jnp.exp2(shift - top) for shift in shifts]
    summed = sum((s[0:1] + s[1:2]) * scale for s, scale in zip(stats, scales))
    velocity = sum(share[:CH, :].astype(F32) * scale for share, scale in zip(shares, scales))
    return velocity, summed, top


def add_kernel(here_ref, there_ref, out_ref):
    velocity, summed, top = added([here_ref[0], there_ref[0]])
    out_ref[0, :CH, :] = velocity.astype(BF16)
    tail = split_two(summed) + split_two(top)
    filler = jnp.zeros((out_ref.shape[1] - CH - len(tail), out_ref.shape[2]), F32)
    out_ref[0, CH:, :] = jnp.concatenate(tail + (filler,), axis=0).astype(BF16)


def combine_kernel(gain_ref, here_ref, there_ref, beside_ref, out_ref):
    half = out_ref.shape[2]
    velocity, summed, _ = added([here_ref[0], there_ref[0], beside_ref[0]])
    velocity = (velocity * (gain_ref[0] / summed)).T
    velocity = velocity.reshape(out_ref.shape[0], 2, half, CH)
    velocity = jnp.concatenate([velocity[:, 0], velocity[:, 1]], axis=2).astype(BF16)
    for side in range(out_ref.shape[1]):
        out_ref[:, side] = velocity


def body(
    query_main, key_main, value_main, query_guide, key_guide, value_guide, map_main, map_guide
):
    tokens_here = query_main.shape[0]
    main_heads = query_main.shape[1] // HD
    guide_heads = query_guide.shape[1] // HD
    heads = main_heads + guide_heads
    head = lax.axis_index("zh")

    maps = jnp.concatenate([map_main, map_guide], axis=0).reshape(-1, HD, CH)
    map_t = lax.dynamic_index_in_dim(maps, head, 0, keepdims=False).T
    gain = jnp.where(head < main_heads, guidance, 1.0 - guidance).astype(F32).reshape(1)

    with jax.named_scope("pack"):
        packed = pl.pallas_call(
            functools.partial(pack_kernel, main_heads, guide_heads),
            in_specs=[VMEM] * 6,
            out_specs=VMEM,
            out_shape=jax.ShapeDtypeStruct((heads, 3, tokens_here, HD), BF16),
        )(query_main, key_main, value_main, query_guide, key_guide, value_guide)
    with jax.named_scope("to_heads"):
        arrived = exchange(packed, Z, PLANE_SETS)
    with jax.named_scope("gather"):
        copies = (len(KEY_SETS[0]), heads, 2, tokens_here, HD)
        q, copies = pl.pallas_call(
            copy_kernel,
            in_specs=[VMEM],
            out_specs=[VMEM] * 2,
            out_shape=[
                jax.ShapeDtypeStruct((heads * tokens_here, HD), BF16),
                jax.ShapeDtypeStruct(copies, BF16),
            ],
            compiler_params=SMALL,
        )(arrived)
        key_values = exchange(copies.reshape((-1,) + copies.shape[2:]), KEY_AXES, KEY_SETS)
        beside = from_partner(q, Z0_STEP)
        across = [from_partner(q, Y_STEP), from_partner(q, Y_STEP ^ Z0_STEP)]
    with jax.named_scope("attend"):
        first, second = across[1], across[0]
        first_share = attend([first], key_values, map_t)
        second, first_share = lax.optimization_barrier((second, first_share))
        there_beside = from_partner(first_share, Y_STEP)
        there = from_partner(attend([second], key_values, map_t), Y_STEP)
        share = pl.pallas_call(
            add_kernel,
            in_specs=[VMEM] * 2,
            out_specs=VMEM,
            out_shape=jax.ShapeDtypeStruct(there.shape, BF16),
            compiler_params=SMALL,
        )(attend([beside], key_values, map_t), there_beside)
        here_beside = from_partner(share, Z0_STEP)
        here = attend([q], key_values, map_t)
    with jax.named_scope("combine"):
        velocity = pl.pallas_call(
            combine_kernel,
            in_specs=[SMEM] + [VMEM] * 3,
            out_specs=VMEM,
            out_shape=jax.ShapeDtypeStruct((heads, SIDES, tokens_here // 2, 2 * CH), BF16),
            compiler_params=SMALL,
        )(gain, here, there, here_beside)
    with jax.named_scope("to_tokens"):
        velocity = velocity.reshape((heads * SIDES,) + velocity.shape[2:])
        velocity = exchange(velocity, PLANE_AXES, SIDE_SETS)
        velocity = jnp.sum(velocity.astype(F32), axis=0)
        velocity = jnp.sum(lax.all_gather(velocity, "c", axis=0), axis=0)
    return velocity.reshape(tokens_here // 2, 2, CH).transpose(1, 0, 2).reshape(tokens_here, CH)


def solution(mesh):
    fine = Mesh(mesh.devices.reshape(4, 8, 2, 2, 2, 2), SEQ + GRP)
    placed = (P(SEQ, GRP),) * 6 + (P(GRP, None),) * 2
    return jax.shard_map(
        body, mesh=fine, in_specs=placed, out_specs=P(SEQ, None), check_vma=False
    )
```

```python
import functools
import math

import jax
import jax.numpy as jnp
from jax import lax
from jax.experimental import pallas as pl
from jax.experimental.pallas import tpu as pltpu
from jax.sharding import Mesh
from jax.sharding import PartitionSpec as P

HD = 128
CH = 64
guidance = 2.5
SCALE = math.log2(math.e) / math.sqrt(HD)
F32 = jnp.float32
BF16 = jnp.bfloat16
VMEM = pl.BlockSpec(memory_space=pltpu.VMEM)
SMEM = pl.BlockSpec(memory_space=pltpu.SMEM)
SMALL = pltpu.CompilerParams(vmem_limit_bytes=12 << 20)
MESSAGE_ROWS = CH + 16

SEQ = ("y", "zh", "z0", "xl")
GRP = ("xh", "c")
Z = ("zh", "z0")
PLANE_SETS = ([0, 2, 4, 6, 9, 11, 13, 15], [1, 3, 5, 7, 8, 10, 12, 14])
QUERY_AXES = ("y", "xl")
X_STEP, Y_STEP = 1, 2
KEY_AXES = ("y", "z0")
KEY_SETS = ([0, 1, 6, 7], [2, 3, 4, 5])
SIDES = 2
PLANE_AXES = Z + ("xh",)
SIDE_SETS = [[SIDES * z + x for z in planes for x in range(SIDES)] for planes in PLANE_SETS]


def exchange(x, axes, sets):
    return lax.all_to_all(x, axes, 0, 0, tiled=True, axis_index_groups=sets)


def from_partner(x, step):
    size = lax.axis_size(QUERY_AXES)
    return lax.ppermute(x, QUERY_AXES, [(i, i ^ step) for i in range(size)])


def dot_t(a, b):
    return lax.dot_general(a, b, (((1,), (1,)), ((), ())), preferred_element_type=F32)


def pack_kernel(main_heads, guide_heads, qm, km, vm, qg, kg, vg, out_ref):
    for h in range(main_heads + guide_heads):
        at = (h if h < main_heads else h - main_heads) * HD
        for t, ref in enumerate((qm, km, vm) if h < main_heads else (qg, kg, vg)):
            out_ref[h, t] = ref[:, at : at + HD]


def copy_kernel(in_ref, q_ref, copies_ref):
    heads, _, tokens, _ = in_ref.shape
    for h in range(heads):
        q_ref[h * tokens : (h + 1) * tokens, :] = in_ref[h, 0]
        for copy in range(copies_ref.shape[0]):
            copies_ref[copy, h] = in_ref[h, 1:]


def split_two(x):
    high = x.astype(BF16).astype(F32)
    return high, x - high


def message(velocity, summed, top, rows, dtype):
    tail = split_two(summed) + split_two(top) if dtype == BF16 else (summed, top)
    filler = jnp.zeros((rows - CH - len(tail), velocity.shape[1]), F32)
    return jnp.concatenate((velocity,) + tail + (filler,), axis=0).astype(dtype)


def attend_kernel(count, first_before, *refs):
    q_refs, refs = refs[:count], refs[count:]
    if first_before is None:
        arrived_ref, map_ref, out_ref, staged_ref, sums_ref = refs
        before_ref = None
    else:
        own_ref, kv_ref, map_ref, before_ref, out_ref, staged_ref, sums_ref = refs
    rows = out_ref.shape[2]
    for k, q_ref in enumerate(q_refs):
        staged_ref[k] = q_ref[...]

    def all_pieces(which):
        if first_before is None:
            return arrived_ref[:, 1 + which].reshape(-1, HD)
        blocks = len(KEY_SETS[0])
        size = kv_ref.shape[0] // blocks
        starts = [(own_ref[0] ^ i) * size for i in range(1, blocks)]
        pieces = [kv_ref[pl.ds(start, size), which].reshape(-1, HD) for start in starts]
        return jnp.concatenate(pieces, axis=0)

    def weighted(queries, shift):
        scores = dot_t(queries, all_pieces(0)) * SCALE
        if shift is not None:
            scores = scores - shift
        values = all_pieces(1)
        values = jnp.concatenate([values, jnp.ones_like(values)], axis=1)
        weights = jnp.exp2(scores).astype(BF16)
        return jnp.dot(weights, values, preferred_element_type=F32)

    def emit(k, at, total, shift):
        count = total.shape[0]
        lane = lax.broadcasted_iota(jnp.int32, (count, HD), 1)
        picks = lax.broadcasted_iota(jnp.int32, (16, HD), 0) == lax.broadcasted_iota(
            jnp.int32, (16, HD), 1
        )
        velocity = dot_t(map_ref[...], total[:, :HD].astype(BF16))
        high, low = split_two(total[:, HD:])
        rest = jnp.where(lane == 0, high, jnp.where(lane == 1, low, 0.0))
        if shift is not None:
            high, low = split_two(shift)
            rest = jnp.where(lane == 2, high, jnp.where(lane == 3, low, rest))
        rest = dot_t(picks.astype(F32).astype(BF16), rest.astype(BF16))
        summed, top = rest[0:1] + rest[1:2], rest[2:3] + rest[3:4]
        if before_ref is not None:
            before = before_ref[first_before + k, :, at]
            velocity, summed, top = joined(
                [velocity, before[:CH]], [summed, before[CH : CH + 1]], [top, before[CH + 1 : CH + 2]]
            )
        out_ref[k, :, at] = message(velocity, summed, top, out_ref.shape[1], out_ref.dtype)

    @pl.loop(0, len(q_refs))
    def _(k):
        total = weighted(staged_ref[k], None)
        emit(k, slice(None), total, None)
        sums_ref[...] = total[:, HD:]
        least = jnp.min(sums_ref[...])
        most = jnp.max(sums_ref[...])

        @pl.when(jnp.logical_not((least > 1e-20) & (most < 1e25)))
        def _():
            @pl.loop(0, rows // HD)
            def _(i):
                at = pl.ds(pl.multiple_of(i * HD, HD), HD)
                queries = staged_ref[k, at, :]
                top = jnp.max(dot_t(queries, all_pieces(0)), axis=1, keepdims=True)
                shift = jnp.ceil(top * SCALE)
                emit(k, at, weighted(queries, shift), shift)


def attend(queries, keys_in, map_t, first_before=None):
    rows = queries[0].shape[0]
    blocks = len(queries)
    last = first_before is not None
    keys = rows * (len(KEY_SETS[0]) - 1 if last else 1)
    operands = [*queries, *keys_in[:2], map_t, *keys_in[2:]]
    specs = [VMEM] * len(operands)
    if last:
        specs[blocks] = SMEM
    out = (blocks, MESSAGE_ROWS, rows) if last else (blocks, CH + 8, rows)
    return pl.pallas_call(
        functools.partial(attend_kernel, blocks, first_before),
        in_specs=specs,
        out_specs=VMEM,
        out_shape=jax.ShapeDtypeStruct(out, BF16 if last else F32),
        scratch_shapes=[pltpu.VMEM((blocks, rows, HD), BF16), pltpu.VMEM((rows, HD), F32)],
        compiler_params=pltpu.CompilerParams(vmem_limit_bytes=28 << 20),
        cost_estimate=pl.CostEstimate(
            flops=8 * blocks * rows * keys * HD,
            bytes_accessed=2 << 20,
            transcendentals=blocks * rows * keys,
        ),
    )(*operands)


def joined(velocities, sums, shifts):
    top = functools.reduce(jnp.maximum, shifts)
    scales = [jnp.exp2(shift - top) for shift in shifts]
    summed = sum(s * scale for s, scale in zip(sums, scales))
    velocity = sum(v * scale for v, scale in zip(velocities, scales))
    return velocity, summed, top


def added(shares):
    stats = [share[CH:, :].astype(F32) for share in shares]
    return joined(
        [share[:CH, :].astype(F32) for share in shares],
        [s[0:1] + s[1:2] for s in stats],
        [s[2:3] + s[3:4] for s in stats],
    )


def add_kernel(here_ref, there_ref, out_ref):
    share = added([here_ref[1], there_ref[1]])
    out_ref[...] = message(*share, out_ref.shape[0], BF16)


def combine_kernel(gain_ref, here_ref, there_ref, beside_ref, out_ref):
    half = out_ref.shape[2]
    velocity, summed, _ = added([here_ref[0], there_ref[0], beside_ref[...]])
    velocity = (velocity * (gain_ref[0] / summed)).T
    velocity = velocity.reshape(out_ref.shape[0], 2, half, CH)
    velocity = jnp.concatenate([velocity[:, 0], velocity[:, 1]], axis=2).astype(BF16)
    for side in range(out_ref.shape[1]):
        out_ref[:, side] = velocity


def body(
    query_main, key_main, value_main, query_guide, key_guide, value_guide, map_main, map_guide
):
    tokens_here = query_main.shape[0]
    main_heads = query_main.shape[1] // HD
    guide_heads = query_guide.shape[1] // HD
    heads = main_heads + guide_heads
    head = lax.axis_index("zh")

    maps = jnp.concatenate([map_main, map_guide], axis=0).reshape(-1, HD, CH)
    map_t = lax.dynamic_index_in_dim(maps, head, 0, keepdims=False).T
    gain = jnp.where(head < main_heads, guidance, 1.0 - guidance).astype(F32).reshape(1)

    with jax.named_scope("pack"):
        packed = pl.pallas_call(
            functools.partial(pack_kernel, main_heads, guide_heads),
            in_specs=[VMEM] * 6,
            out_specs=VMEM,
            out_shape=jax.ShapeDtypeStruct((heads, 3, tokens_here, HD), BF16),
        )(query_main, key_main, value_main, query_guide, key_guide, value_guide)
    with jax.named_scope("to_heads"):
        arrived = exchange(packed, Z, PLANE_SETS)
    with jax.named_scope("gather"):
        copies = (len(KEY_SETS[0]), heads, 2, tokens_here, HD)
        q, copies = pl.pallas_call(
            copy_kernel,
            in_specs=[VMEM],
            out_specs=[VMEM] * 2,
            out_shape=[
                jax.ShapeDtypeStruct((heads * tokens_here, HD), BF16),
                jax.ShapeDtypeStruct(copies, BF16),
            ],
            compiler_params=SMALL,
        )(arrived)
        key_values = exchange(copies.reshape((-1,) + copies.shape[2:]), KEY_AXES, KEY_SETS)
        beside = from_partner(q, X_STEP)
        across = [from_partner(q, Y_STEP), from_partner(q, Y_STEP ^ X_STEP)]
    with jax.named_scope("attend"):
        before = attend(across + [q, beside], [arrived], map_t)
        own = ((lax.axis_index("y") >> 1) * 2 + lax.axis_index("z0")).astype(jnp.int32)
        others = [own.reshape(1), key_values, before]
        there = from_partner(attend(across, others, map_t, 0), Y_STEP)
        here = attend([q, beside], others, map_t, len(across))
    with jax.named_scope("combine"):
        share = pl.pallas_call(
            add_kernel,
            in_specs=[VMEM] * 2,
            out_specs=VMEM,
            out_shape=jax.ShapeDtypeStruct(here.shape[1:], BF16),
            compiler_params=SMALL,
        )(here, there)
        velocity = pl.pallas_call(
            combine_kernel,
            in_specs=[SMEM] + [VMEM] * 3,
            out_specs=VMEM,
            out_shape=jax.ShapeDtypeStruct((heads, SIDES, tokens_here // 2, 2 * CH), BF16),
            compiler_params=SMALL,
        )(gain, here, there, from_partner(share, X_STEP))
    with jax.named_scope("to_tokens"):
        velocity = velocity.reshape((heads * SIDES,) + velocity.shape[2:])
        velocity = exchange(velocity, PLANE_AXES, SIDE_SETS)
        velocity = jnp.sum(velocity.astype(F32), axis=0)
        velocity = jnp.sum(lax.all_gather(velocity, "c", axis=0), axis=0)
    return velocity.reshape(tokens_here // 2, 2, CH).transpose(1, 0, 2).reshape(tokens_here, CH)


def solution(mesh):
    fine = Mesh(mesh.devices.reshape(4, 8, 2, 2, 2, 2), SEQ + GRP)
    placed = (P(SEQ, GRP),) * 6 + (P(GRP, None),) * 2
    return jax.shard_map(
        body, mesh=fine, in_specs=placed, out_specs=P(SEQ, None), check_vma=False
    )
```

```python
import functools
import math

import jax
import jax.numpy as jnp
from jax import lax
from jax.experimental import pallas as pl
from jax.experimental.pallas import tpu as pltpu
from jax.sharding import Mesh
from jax.sharding import PartitionSpec as P

HD = 128
CH = 64
guidance = 2.5
SCALE = math.log2(math.e) / math.sqrt(HD)
F32 = jnp.float32
BF16 = jnp.bfloat16
VMEM = pl.BlockSpec(memory_space=pltpu.VMEM)
SMEM = pl.BlockSpec(memory_space=pltpu.SMEM)
SMALL = pltpu.CompilerParams(vmem_limit_bytes=12 << 20)
MESSAGE_ROWS = CH + 16

SEQ = ("y", "zh", "z0", "xl")
GRP = ("xh", "c")
Z = ("zh", "z0")
PLANE_SETS = ([0, 2, 4, 6, 9, 11, 13, 15], [1, 3, 5, 7, 8, 10, 12, 14])
QUERY_AXES = ("y", "xl")
X_STEP, Y_STEP = 1, 2
KEY_AXES = ("y", "z0")
KEY_SETS = ([0, 1, 6, 7], [2, 3, 4, 5])
SIDES = 2
PLANE_AXES = Z + ("xh",)
SIDE_SETS = [[SIDES * z + x for z in planes for x in range(SIDES)] for planes in PLANE_SETS]


def exchange(x, axes, sets):
    return lax.all_to_all(x, axes, 0, 0, tiled=True, axis_index_groups=sets)


def from_partner(x, step):
    size = lax.axis_size(QUERY_AXES)
    return lax.ppermute(x, QUERY_AXES, [(i, i ^ step) for i in range(size)])


def dot_t(a, b):
    return lax.dot_general(a, b, (((1,), (1,)), ((), ())), preferred_element_type=F32)


def pack_kernel(main_heads, guide_heads, qm, km, vm, qg, kg, vg, out_ref):
    for h in range(main_heads + guide_heads):
        at = (h if h < main_heads else h - main_heads) * HD
        for t, ref in enumerate((qm, km, vm) if h < main_heads else (qg, kg, vg)):
            out_ref[h, t] = ref[:, at : at + HD]


def copy_kernel(in_ref, q_ref, copies_ref):
    heads, _, tokens, _ = in_ref.shape
    for h in range(heads):
        q_ref[h * tokens : (h + 1) * tokens, :] = in_ref[h, 0]
        for copy in range(copies_ref.shape[0]):
            copies_ref[copy, h] = in_ref[h, 1:]


def split_two(x):
    high = x.astype(BF16).astype(F32)
    return high, x - high


def message(velocity, summed, top, rows, dtype):
    tail = split_two(summed) + split_two(top) if dtype == BF16 else (summed, top)
    filler = jnp.zeros((rows - CH - len(tail), velocity.shape[1]), F32)
    return jnp.concatenate((velocity,) + tail + (filler,), axis=0).astype(dtype)


def attend_kernel(count, first_before, *refs):
    q_refs, refs = refs[:count], refs[count:]
    if first_before is None:
        arrived_ref, map_ref, out_ref, staged_ref, sums_ref = refs
        before_ref = None
    else:
        own_ref, kv_ref, map_ref, before_ref, out_ref, staged_ref, sums_ref = refs
    rows = out_ref.shape[2]
    for k, q_ref in enumerate(q_refs):
        staged_ref[k] = q_ref[...]

    def all_pieces(which):
        if first_before is None:
            return arrived_ref[:, 1 + which].reshape(-1, HD)
        blocks = len(KEY_SETS[0])
        size = kv_ref.shape[0] // blocks
        starts = [(own_ref[0] ^ i) * size for i in range(1, blocks)]
        pieces = [kv_ref[pl.ds(start, size), which].reshape(-1, HD) for start in starts]
        return jnp.concatenate(pieces, axis=0)

    def weighted(queries, shift):
        scores = dot_t(queries, all_pieces(0)) * SCALE
        if shift is not None:
            scores = scores - shift
        values = all_pieces(1)
        values = jnp.concatenate([values, jnp.ones_like(values)], axis=1)
        weights = jnp.exp2(scores).astype(BF16)
        return jnp.dot(weights, values, preferred_element_type=F32)

    def emit(k, at, total, shift):
        count = total.shape[0]
        lane = lax.broadcasted_iota(jnp.int32, (count, HD), 1)
        picks = lax.broadcasted_iota(jnp.int32, (16, HD), 0) == lax.broadcasted_iota(
            jnp.int32, (16, HD), 1
        )
        velocity = dot_t(map_ref[...], total[:, :HD].astype(BF16))
        high, low = split_two(total[:, HD:])
        rest = jnp.where(lane == 0, high, jnp.where(lane == 1, low, 0.0))
        if shift is not None:
            high, low = split_two(shift)
            rest = jnp.where(lane == 2, high, jnp.where(lane == 3, low, rest))
        rest = dot_t(picks.astype(F32).astype(BF16), rest.astype(BF16))
        summed, top = rest[0:1] + rest[1:2], rest[2:3] + rest[3:4]
        if before_ref is not None:
            before = before_ref[first_before + k, :, at]
            velocity, summed, top = joined(
                [velocity, before[:CH]], [summed, before[CH : CH + 1]], [top, before[CH + 1 : CH + 2]]
            )
        out_ref[k, :, at] = message(velocity, summed, top, out_ref.shape[1], out_ref.dtype)

    @pl.loop(0, len(q_refs))
    def _(k):
        total = weighted(staged_ref[k], None)
        emit(k, slice(None), total, None)
        sums_ref[...] = total[:, HD:]
        least = jnp.min(sums_ref[...])
        most = jnp.max(sums_ref[...])

        @pl.when(jnp.logical_not((least > 1e-20) & (most < 1e25)))
        def _():
            @pl.loop(0, rows // HD)
            def _(i):
                at = pl.ds(pl.multiple_of(i * HD, HD), HD)
                queries = staged_ref[k, at, :]
                top = jnp.max(dot_t(queries, all_pieces(0)), axis=1, keepdims=True)
                shift = jnp.ceil(top * SCALE)
                emit(k, at, weighted(queries, shift), shift)


def attend(queries, keys_in, map_t, first_before=None):
    rows = queries[0].shape[0]
    blocks = len(queries)
    last = first_before is not None
    keys = rows * (len(KEY_SETS[0]) - 1 if last else 1)
    operands = [*queries, *keys_in[:2], map_t, *keys_in[2:]]
    specs = [VMEM] * len(operands)
    if last:
        specs[blocks] = SMEM
    out = (blocks, MESSAGE_ROWS, rows) if last else (blocks, CH + 8, rows)
    return pl.pallas_call(
        functools.partial(attend_kernel, blocks, first_before),
        in_specs=specs,
        out_specs=VMEM,
        out_shape=jax.ShapeDtypeStruct(out, BF16 if last else F32),
        scratch_shapes=[pltpu.VMEM((blocks, rows, HD), BF16), pltpu.VMEM((rows, HD), F32)],
        compiler_params=pltpu.CompilerParams(vmem_limit_bytes=28 << 20),
        cost_estimate=pl.CostEstimate(
            flops=8 * blocks * rows * keys * HD,
            bytes_accessed=2 << 20,
            transcendentals=blocks * rows * keys,
        ),
    )(*operands)


def joined(velocities, sums, shifts):
    top = functools.reduce(jnp.maximum, shifts)
    scales = [jnp.exp2(shift - top) for shift in shifts]
    summed = sum(s * scale for s, scale in zip(sums, scales))
    velocity = sum(v * scale for v, scale in zip(velocities, scales))
    return velocity, summed, top


def added(shares):
    stats = [share[CH:, :].astype(F32) for share in shares]
    return joined(
        [share[:CH, :].astype(F32) for share in shares],
        [s[0:1] + s[1:2] for s in stats],
        [s[2:3] + s[3:4] for s in stats],
    )


def add_kernel(here_ref, there_ref, out_ref):
    share = added([here_ref[1], there_ref[1]])
    out_ref[...] = message(*share, out_ref.shape[0], BF16)


def combine_kernel(gain_ref, here_ref, there_ref, beside_ref, out_ref):
    half = out_ref.shape[2]
    velocity, summed, _ = added([here_ref[0], there_ref[0], beside_ref[...]])
    velocity = (velocity * (gain_ref[0] / summed)).T
    velocity = velocity.reshape(out_ref.shape[0], 2, half, CH)
    velocity = jnp.concatenate([velocity[:, 0], velocity[:, 1]], axis=2).astype(BF16)
    for side in range(out_ref.shape[1]):
        out_ref[:, side] = velocity


def body(
    query_main, key_main, value_main, query_guide, key_guide, value_guide, map_main, map_guide
):
    tokens_here = query_main.shape[0]
    main_heads = query_main.shape[1] // HD
    guide_heads = query_guide.shape[1] // HD
    heads = main_heads + guide_heads
    head = lax.axis_index("zh")

    maps = jnp.concatenate([map_main, map_guide], axis=0).reshape(-1, HD, CH)
    map_t = lax.dynamic_index_in_dim(maps, head, 0, keepdims=False).T
    gain = jnp.where(head < main_heads, guidance, 1.0 - guidance).astype(F32).reshape(1)

    with jax.named_scope("pack"):
        packed = pl.pallas_call(
            functools.partial(pack_kernel, main_heads, guide_heads),
            in_specs=[VMEM] * 6,
            out_specs=VMEM,
            out_shape=jax.ShapeDtypeStruct((heads, 3, tokens_here, HD), BF16),
        )(query_main, key_main, value_main, query_guide, key_guide, value_guide)
    with jax.named_scope("to_heads"):
        arrived = exchange(packed, Z, PLANE_SETS)
    with jax.named_scope("gather"):
        copies = (len(KEY_SETS[0]), heads, 2, tokens_here, HD)
        q, copies = pl.pallas_call(
            copy_kernel,
            in_specs=[VMEM],
            out_specs=[VMEM] * 2,
            out_shape=[
                jax.ShapeDtypeStruct((heads * tokens_here, HD), BF16),
                jax.ShapeDtypeStruct(copies, BF16),
            ],
            compiler_params=SMALL,
        )(arrived)
        key_values = exchange(copies.reshape((-1,) + copies.shape[2:]), KEY_AXES, KEY_SETS)
        beside = from_partner(q, X_STEP)
        across = [from_partner(q, Y_STEP), from_partner(q, Y_STEP ^ X_STEP)]
    with jax.named_scope("attend"):
        ours = [q, beside]
        before_across = attend(across, [arrived], map_t)
        before_ours = attend(ours, [arrived], map_t)
        own = ((lax.axis_index("y") >> 1) * 2 + lax.axis_index("z0")).astype(jnp.int32)
        others = [own.reshape(1), key_values]
        there = from_partner(attend(across, others + [before_across], map_t, 0), Y_STEP)
        here = attend(ours, others + [before_ours], map_t, 0)
    with jax.named_scope("combine"):
        share = pl.pallas_call(
            add_kernel,
            in_specs=[VMEM] * 2,
            out_specs=VMEM,
            out_shape=jax.ShapeDtypeStruct(here.shape[1:], BF16),
            compiler_params=SMALL,
        )(here, there)
        velocity = pl.pallas_call(
            combine_kernel,
            in_specs=[SMEM] + [VMEM] * 3,
            out_specs=VMEM,
            out_shape=jax.ShapeDtypeStruct((heads, SIDES, tokens_here // 2, 2 * CH), BF16),
            compiler_params=SMALL,
        )(gain, here, there, from_partner(share, X_STEP))
    with jax.named_scope("to_tokens"):
        velocity = velocity.reshape((heads * SIDES,) + velocity.shape[2:])
        velocity = exchange(velocity, PLANE_AXES, SIDE_SETS)
        velocity = jnp.sum(velocity.astype(F32), axis=0)
        velocity = jnp.sum(lax.all_gather(velocity, "c", axis=0), axis=0)
    return velocity.reshape(tokens_here // 2, 2, CH).transpose(1, 0, 2).reshape(tokens_here, CH)


def solution(mesh):
    fine = Mesh(mesh.devices.reshape(4, 8, 2, 2, 2, 2), SEQ + GRP)
    placed = (P(SEQ, GRP),) * 6 + (P(GRP, None),) * 2
    return jax.shard_map(
        body, mesh=fine, in_specs=placed, out_specs=P(SEQ, None), check_vma=False
    )
```

```python
import functools
import math

import jax
import jax.numpy as jnp
from jax import lax
from jax.experimental import pallas as pl
from jax.experimental.pallas import tpu as pltpu
from jax.sharding import Mesh
from jax.sharding import PartitionSpec as P

HD = 128
CH = 64
guidance = 2.5
SCALE = math.log2(math.e) / math.sqrt(HD)
F32 = jnp.float32
BF16 = jnp.bfloat16
VMEM = pl.BlockSpec(memory_space=pltpu.VMEM)
SMEM = pl.BlockSpec(memory_space=pltpu.SMEM)
SMALL = pltpu.CompilerParams(vmem_limit_bytes=12 << 20)
MESSAGE_ROWS = CH + 16

SEQ = ("y", "zh", "z0", "xl")
GRP = ("xh", "c")
Z = ("zh", "z0")
PLANE_SETS = ([0, 2, 4, 6, 9, 11, 13, 15], [1, 3, 5, 7, 8, 10, 12, 14])
QUERY_AXES = ("y", "xl")
X_STEP, Y_STEP = 1, 2
KEY_AXES = ("y", "z0")
KEY_SETS = ([0, 1, 6, 7], [2, 3, 4, 5])
SIDES = 2
PLANE_AXES = Z + ("xh",)
SIDE_SETS = [[SIDES * z + x for z in planes for x in range(SIDES)] for planes in PLANE_SETS]


def exchange(x, axes, sets):
    return lax.all_to_all(x, axes, 0, 0, tiled=True, axis_index_groups=sets)


def from_partner(x, step):
    size = lax.axis_size(QUERY_AXES)
    return lax.ppermute(x, QUERY_AXES, [(i, i ^ step) for i in range(size)])


def dot_t(a, b):
    return lax.dot_general(a, b, (((1,), (1,)), ((), ())), preferred_element_type=F32)


def pack_kernel(main_heads, guide_heads, qm, km, vm, qg, kg, vg, out_ref, done):
    copies = []
    for h in range(main_heads + guide_heads):
        at = (h if h < main_heads else h - main_heads) * HD
        for t, ref in enumerate((qm, km, vm) if h < main_heads else (qg, kg, vg)):
            source = ref.at[:, at : at + HD]
            copies.append(pltpu.make_async_copy(source, out_ref.at[h, t], done.at[h, t]))
    for copy in copies:
        copy.start()
    for copy in copies:
        copy.wait()


def copy_kernel(in_ref, q_ref, copies_ref):
    heads, _, tokens, _ = in_ref.shape
    for h in range(heads):
        q_ref[h * tokens : (h + 1) * tokens, :] = in_ref[h, 0]
        for copy in range(copies_ref.shape[0]):
            copies_ref[copy, h] = in_ref[h, 1:]


def split_two(x):
    high = x.astype(BF16).astype(F32)
    return high, x - high


def message(velocity, summed, top, rows, dtype):
    tail = split_two(summed) + split_two(top) if dtype == BF16 else (summed, top)
    filler = jnp.zeros((rows - CH - len(tail), velocity.shape[1]), F32)
    return jnp.concatenate((velocity,) + tail + (filler,), axis=0).astype(dtype)


def attend_kernel(count, first_before, *refs):
    q_refs, refs = refs[:count], refs[count:]
    if first_before is None:
        arrived_ref, map_ref, out_ref, staged_ref, sums_ref = refs
        before_ref = None
    else:
        own_ref, kv_ref, map_ref, before_ref, out_ref, staged_ref, sums_ref = refs
    rows = out_ref.shape[2]
    for k, q_ref in enumerate(q_refs):
        staged_ref[k] = q_ref[...]

    def all_pieces(which):
        if first_before is None:
            return arrived_ref[:, 1 + which].reshape(-1, HD)
        blocks = len(KEY_SETS[0])
        size = kv_ref.shape[0] // blocks
        starts = [(own_ref[0] ^ i) * size for i in range(1, blocks)]
        pieces = [kv_ref[pl.ds(start, size), which].reshape(-1, HD) for start in starts]
        return jnp.concatenate(pieces, axis=0)

    def weighted(queries, shift):
        scores = dot_t(queries, all_pieces(0)) * SCALE
        if shift is not None:
            scores = scores - shift
        values = all_pieces(1)
        values = jnp.concatenate([values, jnp.ones_like(values)], axis=1)
        weights = jnp.exp2(scores).astype(BF16)
        return jnp.dot(weights, values, preferred_element_type=F32)

    def emit(k, at, total, shift):
        count = total.shape[0]
        lane = lax.broadcasted_iota(jnp.int32, (count, HD), 1)
        picks = lax.broadcasted_iota(jnp.int32, (16, HD), 0) == lax.broadcasted_iota(
            jnp.int32, (16, HD), 1
        )
        velocity = dot_t(map_ref[...], total[:, :HD].astype(BF16))
        high, low = split_two(total[:, HD:])
        rest = jnp.where(lane == 0, high, jnp.where(lane == 1, low, 0.0))
        if shift is not None:
            high, low = split_two(shift)
            rest = jnp.where(lane == 2, high, jnp.where(lane == 3, low, rest))
        rest = dot_t(picks.astype(F32).astype(BF16), rest.astype(BF16))
        summed, top = rest[0:1] + rest[1:2], rest[2:3] + rest[3:4]
        if before_ref is not None:
            before = before_ref[first_before + k, :, at]
            velocity, summed, top = joined(
                [velocity, before[:CH]], [summed, before[CH : CH + 1]], [top, before[CH + 1 : CH + 2]]
            )
        out_ref[k, :, at] = message(velocity, summed, top, out_ref.shape[1], out_ref.dtype)

    @pl.loop(0, len(q_refs))
    def _(k):
        total = weighted(staged_ref[k], None)
        emit(k, slice(None), total, None)
        sums_ref[...] = total[:, HD:]
        least = jnp.min(sums_ref[...])
        most = jnp.max(sums_ref[...])

        @pl.when(jnp.logical_not((least > 1e-20) & (most < 1e25)))
        def _():
            @pl.loop(0, rows // HD)
            def _(i):
                at = pl.ds(pl.multiple_of(i * HD, HD), HD)
                queries = staged_ref[k, at, :]
                top = jnp.max(dot_t(queries, all_pieces(0)), axis=1, keepdims=True)
                shift = jnp.ceil(top * SCALE)
                emit(k, at, weighted(queries, shift), shift)


def attend(queries, keys_in, map_t, first_before=None):
    rows = queries[0].shape[0]
    blocks = len(queries)
    last = first_before is not None
    keys = rows * (len(KEY_SETS[0]) - 1 if last else 1)
    operands = [*queries, *keys_in[:2], map_t, *keys_in[2:]]
    specs = [VMEM] * len(operands)
    if last:
        specs[blocks] = SMEM
    out = (blocks, MESSAGE_ROWS, rows) if last else (blocks, CH + 8, rows)
    return pl.pallas_call(
        functools.partial(attend_kernel, blocks, first_before),
        in_specs=specs,
        out_specs=VMEM,
        out_shape=jax.ShapeDtypeStruct(out, BF16 if last else F32),
        scratch_shapes=[pltpu.VMEM((blocks, rows, HD), BF16), pltpu.VMEM((rows, HD), F32)],
        compiler_params=pltpu.CompilerParams(vmem_limit_bytes=28 << 20),
        cost_estimate=pl.CostEstimate(
            flops=8 * blocks * rows * keys * HD,
            bytes_accessed=2 << 20,
            transcendentals=blocks * rows * keys,
        ),
    )(*operands)


def joined(velocities, sums, shifts):
    top = functools.reduce(jnp.maximum, shifts)
    scales = [jnp.exp2(shift - top) for shift in shifts]
    summed = sum(s * scale for s, scale in zip(sums, scales))
    velocity = sum(v * scale for v, scale in zip(velocities, scales))
    return velocity, summed, top


def added(shares):
    stats = [share[CH:, :].astype(F32) for share in shares]
    return joined(
        [share[:CH, :].astype(F32) for share in shares],
        [s[0:1] + s[1:2] for s in stats],
        [s[2:3] + s[3:4] for s in stats],
    )


def add_kernel(here_ref, there_ref, out_ref):
    share = added([here_ref[1], there_ref[1]])
    out_ref[...] = message(*share, out_ref.shape[0], BF16)


def combine_kernel(gain_ref, here_ref, there_ref, beside_ref, out_ref):
    half = out_ref.shape[2]
    velocity, summed, _ = added([here_ref[0], there_ref[0], beside_ref[...]])
    velocity = (velocity * (gain_ref[0] / summed)).T
    velocity = velocity.reshape(out_ref.shape[0], 2, half, CH)
    velocity = jnp.concatenate([velocity[:, 0], velocity[:, 1]], axis=2).astype(BF16)
    for side in range(out_ref.shape[1]):
        out_ref[:, side] = velocity


def body(
    query_main, key_main, value_main, query_guide, key_guide, value_guide, map_main, map_guide
):
    tokens_here = query_main.shape[0]
    main_heads = query_main.shape[1] // HD
    guide_heads = query_guide.shape[1] // HD
    heads = main_heads + guide_heads
    head = lax.axis_index("zh")

    maps = jnp.concatenate([map_main, map_guide], axis=0).reshape(-1, HD, CH)
    map_t = lax.dynamic_index_in_dim(maps, head, 0, keepdims=False).T
    gain = jnp.where(head < main_heads, guidance, 1.0 - guidance).astype(F32).reshape(1)

    with jax.named_scope("pack"):
        packed = pl.pallas_call(
            functools.partial(pack_kernel, main_heads, guide_heads),
            in_specs=[pl.BlockSpec(memory_space=pl.ANY)] * 6,
            out_specs=pl.BlockSpec(memory_space=pl.ANY),
            out_shape=jax.ShapeDtypeStruct((heads, 3, tokens_here, HD), BF16),
            scratch_shapes=[pltpu.SemaphoreType.DMA((heads, 3))],
        )(query_main, key_main, value_main, query_guide, key_guide, value_guide)
    with jax.named_scope("to_heads"):
        arrived = exchange(packed, Z, PLANE_SETS)
    with jax.named_scope("gather"):
        copies = (len(KEY_SETS[0]), heads, 2, tokens_here, HD)
        q, copies = pl.pallas_call(
            copy_kernel,
            in_specs=[VMEM],
            out_specs=[VMEM] * 2,
            out_shape=[
                jax.ShapeDtypeStruct((heads * tokens_here, HD), BF16),
                jax.ShapeDtypeStruct(copies, BF16),
            ],
            compiler_params=SMALL,
        )(arrived)
        key_values = exchange(copies.reshape((-1,) + copies.shape[2:]), KEY_AXES, KEY_SETS)
        beside = from_partner(q, X_STEP)
        across = [from_partner(q, Y_STEP), from_partner(q, Y_STEP ^ X_STEP)]
    with jax.named_scope("attend"):
        before = attend(across + [q, beside], [arrived], map_t)
        own = ((lax.axis_index("y") >> 1) * 2 + lax.axis_index("z0")).astype(jnp.int32)
        others = [own.reshape(1), key_values, before]
        there = from_partner(attend(across, others, map_t, 0), Y_STEP)
        here = attend([q, beside], others, map_t, len(across))
    with jax.named_scope("combine"):
        share = pl.pallas_call(
            add_kernel,
            in_specs=[VMEM] * 2,
            out_specs=VMEM,
            out_shape=jax.ShapeDtypeStruct(here.shape[1:], BF16),
            compiler_params=SMALL,
        )(here, there)
        velocity = pl.pallas_call(
            combine_kernel,
            in_specs=[SMEM] + [VMEM] * 3,
            out_specs=VMEM,
            out_shape=jax.ShapeDtypeStruct((heads, SIDES, tokens_here // 2, 2 * CH), BF16),
            compiler_params=SMALL,
        )(gain, here, there, from_partner(share, X_STEP))
    with jax.named_scope("to_tokens"):
        velocity = velocity.reshape((heads * SIDES,) + velocity.shape[2:])
        velocity = exchange(velocity, PLANE_AXES, SIDE_SETS)
        velocity = jnp.sum(velocity.astype(F32), axis=0)
        velocity = jnp.sum(lax.all_gather(velocity, "c", axis=0), axis=0)
    return velocity.reshape(tokens_here // 2, 2, CH).transpose(1, 0, 2).reshape(tokens_here, CH)


def solution(mesh):
    fine = Mesh(mesh.devices.reshape(4, 8, 2, 2, 2, 2), SEQ + GRP)
    placed = (P(SEQ, GRP),) * 6 + (P(GRP, None),) * 2
    return jax.shard_map(
        body, mesh=fine, in_specs=placed, out_specs=P(SEQ, None), check_vma=False
    )
```

```python
import functools
import math

import jax
import jax.numpy as jnp
from jax import lax
from jax.experimental import pallas as pl
from jax.experimental.pallas import tpu as pltpu
from jax.sharding import Mesh
from jax.sharding import PartitionSpec as P

HD = 128
CH = 64
guidance = 2.5
SCALE = math.log2(math.e) / math.sqrt(HD)
F32 = jnp.float32
BF16 = jnp.bfloat16
VMEM = pl.BlockSpec(memory_space=pltpu.VMEM)
SMEM = pl.BlockSpec(memory_space=pltpu.SMEM)
SMALL = pltpu.CompilerParams(vmem_limit_bytes=12 << 20)
MESSAGE_ROWS = CH + 16

SEQ = ("y", "zh", "z0", "xl")
GRP = ("xh", "c")
Z = ("zh", "z0")
PLANE_SETS = ([0, 2, 4, 6, 9, 11, 13, 15], [1, 3, 5, 7, 8, 10, 12, 14])
QUERY_AXES = ("y", "xl")
X_STEP, Y_STEP = 1, 2
KEY_AXES = ("y", "z0")
KEY_STEPS = (1, 6, 7)
SIDES = 2
PLANE_AXES = Z + ("xh",)
SIDE_SETS = [[SIDES * z + x for z in planes for x in range(SIDES)] for planes in PLANE_SETS]


def exchange(x, axes, sets):
    return lax.all_to_all(x, axes, 0, 0, tiled=True, axis_index_groups=sets)


def from_partner(x, step, axes=QUERY_AXES):
    return lax.ppermute(x, axes, [(i, i ^ step) for i in range(lax.axis_size(axes))])


def dot_t(a, b):
    return lax.dot_general(a, b, (((1,), (1,)), ((), ())), preferred_element_type=F32)


def pack_kernel(main_heads, guide_heads, qm, km, vm, qg, kg, vg, out_ref):
    for h in range(main_heads + guide_heads):
        at = (h if h < main_heads else h - main_heads) * HD
        for t, ref in enumerate((qm, km, vm) if h < main_heads else (qg, kg, vg)):
            out_ref[h, t] = ref[:, at : at + HD]


def copy_kernel(in_ref, q_ref, kv_ref):
    heads, _, tokens, _ = in_ref.shape
    for h in range(heads):
        q_ref[h * tokens : (h + 1) * tokens, :] = in_ref[h, 0]
        kv_ref[h] = in_ref[h, 1:]


def split_two(x):
    high = x.astype(BF16).astype(F32)
    return high, x - high


def attend_kernel(count, *refs):
    q_refs, refs = refs[:count], refs[count:]
    *kv_refs, map_ref, out_ref, staged_ref, sums_ref = refs
    rows = out_ref.shape[2]
    for k, q_ref in enumerate(q_refs):
        staged_ref[k] = q_ref[...]

    def all_pieces(which):
        return jnp.concatenate([ref[:, which].reshape(-1, HD) for ref in kv_refs], axis=0)

    def weighted(queries, shift):
        scores = dot_t(queries, all_pieces(0)) * SCALE
        if shift is not None:
            scores = scores - shift
        values = all_pieces(1)
        values = jnp.concatenate([values, jnp.ones_like(values)], axis=1)
        weights = jnp.exp2(scores).astype(BF16)
        return jnp.dot(weights, values, preferred_element_type=F32)

    def emit(k, at, total, shift):
        count = total.shape[0]
        lane = lax.broadcasted_iota(jnp.int32, (count, HD), 1)
        picks = lax.broadcasted_iota(jnp.int32, (16, HD), 0) == lax.broadcasted_iota(
            jnp.int32, (16, HD), 1
        )
        out_ref[k, :CH, at] = dot_t(map_ref[...], total[:, :HD].astype(BF16)).astype(BF16)
        high, low = split_two(total[:, HD:])
        rest = jnp.where(lane == 0, high, jnp.where(lane == 1, low, 0.0))
        if shift is not None:
            high, low = split_two(shift)
            rest = jnp.where(lane == 2, high, jnp.where(lane == 3, low, rest))
        rest = dot_t(picks.astype(F32).astype(BF16), rest.astype(BF16))
        out_ref[k, CH:, at] = rest.astype(BF16)

    @pl.loop(0, len(q_refs))
    def _(k):
        total = weighted(staged_ref[k], None)
        emit(k, slice(None), total, None)
        sums_ref[...] = total[:, HD:]
        least = jnp.min(sums_ref[...])
        most = jnp.max(sums_ref[...])

        @pl.when(jnp.logical_not((least > 1e-20) & (most < 1e25)))
        def _():
            @pl.loop(0, rows // HD)
            def _(i):
                at = pl.ds(pl.multiple_of(i * HD, HD), HD)
                queries = staged_ref[k, at, :]
                top = jnp.max(dot_t(queries, all_pieces(0)), axis=1, keepdims=True)
                shift = jnp.ceil(top * SCALE)
                emit(k, at, weighted(queries, shift), shift)


def attend(queries, key_values, map_t):
    rows = queries[0].shape[0]
    keys = key_values[0].shape[0] * key_values[0].shape[2] * len(key_values)
    blocks = len(queries)
    return pl.pallas_call(
        functools.partial(attend_kernel, blocks),
        in_specs=[VMEM] * (1 + blocks + len(key_values)),
        out_specs=VMEM,
        out_shape=jax.ShapeDtypeStruct((blocks, MESSAGE_ROWS, rows), BF16),
        scratch_shapes=[pltpu.VMEM((blocks, rows, HD), BF16), pltpu.VMEM((rows, HD), F32)],
        compiler_params=pltpu.CompilerParams(vmem_limit_bytes=40 << 20),
        cost_estimate=pl.CostEstimate(
            flops=8 * blocks * rows * keys * HD,
            bytes_accessed=2 << 20,
            transcendentals=blocks * rows * keys,
        ),
    )(*queries, *key_values, map_t)


def added(shares):
    stats = [share[CH:, :].astype(F32) for share in shares]
    shifts = [s[2:3] + s[3:4] for s in stats]
    top = functools.reduce(jnp.maximum, shifts)
    scales = [jnp.exp2(shift - top) for shift in shifts]
    summed = sum((s[0:1] + s[1:2]) * scale for s, scale in zip(stats, scales))
    velocity = sum(share[:CH, :].astype(F32) * scale for share, scale in zip(shares, scales))
    return velocity, summed, top


def add_kernel(here_ref, there_ref, out_ref):
    velocity, summed, top = added([here_ref[1], there_ref[1]])
    out_ref[:CH, :] = velocity.astype(BF16)
    tail = split_two(summed) + split_two(top)
    filler = jnp.zeros((out_ref.shape[0] - CH - len(tail), out_ref.shape[1]), F32)
    out_ref[CH:, :] = jnp.concatenate(tail + (filler,), axis=0).astype(BF16)


def combine_kernel(gain_ref, here_ref, there_ref, beside_ref, out_ref):
    half = out_ref.shape[2]
    velocity, summed, _ = added([here_ref[0], there_ref[0], beside_ref[...]])
    velocity = (velocity * (gain_ref[0] / summed)).T
    velocity = velocity.reshape(out_ref.shape[0], 2, half, CH)
    velocity = jnp.concatenate([velocity[:, 0], velocity[:, 1]], axis=2).astype(BF16)
    for side in range(out_ref.shape[1]):
        out_ref[:, side] = velocity


def body(
    query_main, key_main, value_main, query_guide, key_guide, value_guide, map_main, map_guide
):
    tokens_here = query_main.shape[0]
    main_heads = query_main.shape[1] // HD
    guide_heads = query_guide.shape[1] // HD
    heads = main_heads + guide_heads
    head = lax.axis_index("zh")

    maps = jnp.concatenate([map_main, map_guide], axis=0).reshape(-1, HD, CH)
    map_t = lax.dynamic_index_in_dim(maps, head, 0, keepdims=False).T
    gain = jnp.where(head < main_heads, guidance, 1.0 - guidance).astype(F32).reshape(1)

    with jax.named_scope("pack"):
        packed = pl.pallas_call(
            functools.partial(pack_kernel, main_heads, guide_heads),
            in_specs=[VMEM] * 6,
            out_specs=VMEM,
            out_shape=jax.ShapeDtypeStruct((heads, 3, tokens_here, HD), BF16),
        )(query_main, key_main, value_main, query_guide, key_guide, value_guide)
    with jax.named_scope("to_heads"):
        arrived = exchange(packed, Z, PLANE_SETS)
    with jax.named_scope("gather"):
        q, kv = pl.pallas_call(
            copy_kernel,
            in_specs=[VMEM],
            out_specs=[VMEM] * 2,
            out_shape=[
                jax.ShapeDtypeStruct((heads * tokens_here, HD), BF16),
                jax.ShapeDtypeStruct((heads, 2, tokens_here, HD), BF16),
            ],
            compiler_params=SMALL,
        )(arrived)
        key_values = [kv] + [from_partner(kv, step, KEY_AXES) for step in KEY_STEPS]
        beside = from_partner(q, X_STEP)
        across = [from_partner(q, Y_STEP), from_partner(q, Y_STEP ^ X_STEP)]
    with jax.named_scope("attend"):
        there = from_partner(attend(across, key_values, map_t), Y_STEP)
        here = attend([q, beside], key_values, map_t)
    with jax.named_scope("combine"):
        share = pl.pallas_call(
            add_kernel,
            in_specs=[VMEM] * 2,
            out_specs=VMEM,
            out_shape=jax.ShapeDtypeStruct(here.shape[1:], BF16),
            compiler_params=SMALL,
        )(here, there)
        velocity = pl.pallas_call(
            combine_kernel,
            in_specs=[SMEM] + [VMEM] * 3,
            out_specs=VMEM,
            out_shape=jax.ShapeDtypeStruct((heads, SIDES, tokens_here // 2, 2 * CH), BF16),
            compiler_params=SMALL,
        )(gain, here, there, from_partner(share, X_STEP))
    with jax.named_scope("to_tokens"):
        velocity = velocity.reshape((heads * SIDES,) + velocity.shape[2:])
        velocity = exchange(velocity, PLANE_AXES, SIDE_SETS)
        velocity = jnp.sum(velocity.astype(F32), axis=0)
        velocity = jnp.sum(lax.all_gather(velocity, "c", axis=0), axis=0)
    return velocity.reshape(tokens_here // 2, 2, CH).transpose(1, 0, 2).reshape(tokens_here, CH)


def solution(mesh):
    fine = Mesh(mesh.devices.reshape(4, 8, 2, 2, 2, 2), SEQ + GRP)
    placed = (P(SEQ, GRP),) * 6 + (P(GRP, None),) * 2
    return jax.shard_map(
        body, mesh=fine, in_specs=placed, out_specs=P(SEQ, None), check_vma=False
    )
```
